32 devices in a mesh: slab: 4 (over x, core), row: 8 (over z, y).
Axes of the slice: x: 2, y: 2, z: 4, core: 2. Of those that a mesh axis runs over, the one named last changes fastest.
Arguments:
- velocity: bfloat16 [512, 32, 3, 1536], P('row', 'slab'), may hold values from -6 to 6
- deriv_x: bfloat16 [1536, 1536], replicated, may hold values from -0.15625 to 0.15625
- deriv_y: bfloat16 [512, 512], replicated, may hold values from -0.25 to 0.25
- metric_x: float32 [1536], replicated, may hold values from 0.5 to 2
- metric_y: float32 [512], replicated, may hold values from 0.5 to 2
- coarse_force: bfloat16 [128, 16, 3, 192], P('row', 'slab'), may hold values from -6 to 6
- row_map: int32 [512], P('row'), may hold values from 0 to 127, as said below
- x_index: int32 [1536], replicated, may hold values from 0 to 190, as said below
- x_weight: bfloat16 [1536], replicated, may hold values from 0 to 1
Outputs:
- tendency: bfloat16 [512, 32, 3, 1536], P('row', 'slab')
- updated: bfloat16 [512, 32, 3, 1536], P('row', 'slab')
The draws below stay inside these ranges and needn't reach their ends.
Inputs may be any that keep to these rules, and one draw needn't show every extreme that they name: `row_map`: each coarse row is named by exactly 4 fine rows. `x_index`: every value of the range is named by some fine column.
All inputs are finite; a program needn't handle non-finite values.
Results may differ from the reference program's by a relative error of at most 0.004.
Values may be sent and summed in bfloat16 or wider, within the bound.
No kernel may reach another device: no remote copies, remote signals or barrier semaphores. Data moves between devices by JAX's collectives and lax.ppermute only.
A program may use at most 128 MiB of HBM per device.

```python
import math
import jax
import jax.numpy as jnp
from jax import lax

NX = 1536
NY = 512
NYC = 128
NXC = 192
NZ = 32
NZC = 16


def draw_row_map(key, part):
    order = jax.random.permutation(jax.random.fold_in(key, 11), NY)
    return (order % NYC).astype(jnp.int32)


def draw_x_index(key, part):
    order = jax.random.permutation(jax.random.fold_in(key, 23), NX)
    return (order % (NXC - 1)).astype(jnp.int32)


def block_scale(stream_key, extent, pieces, smallest, top_value):
    gain = 1.0
    for axis_at, shards_of in pieces:
        heights = jax.random.uniform(jax.random.fold_in(jax.random.fold_in(stream_key, 6), axis_at), (shards_of,), jnp.float32, smallest / len(pieces), top_value / len(pieces))
        gain = gain * jnp.repeat(jnp.exp(heights), extent[axis_at] // shards_of).reshape((-1,) + (1,) * (len(extent) - 1 - axis_at))
    return gain


def gaussian(own_key, shape, deviation, bound, pieces=(), held_as=jnp.bfloat16):
    loudness = block_scale(own_key, shape, pieces, -0.22, 0.18) if pieces else 1.0
    values = jax.random.normal(own_key, shape, jnp.float32) * deviation * loudness
    return jnp.minimum(jnp.maximum(values, -bound), bound).astype(held_as)


def setup_inputs(seed: int = 0) -> dict:
    streams_of = jax.random.split(jax.random.key(seed), 10)
    return {
        "velocity": gaussian(streams_of[0], (NY, NZ, 3, NX), 1.0, 6.0, ((0, 8), (1, 4))),
        "deriv_x": gaussian(streams_of[1], (NX, NX), NX ** -0.5, 0.15625),
        "deriv_y": gaussian(streams_of[2], (NY, NY), NY ** -0.5, 0.25),
        "metric_x": jnp.clip(jnp.exp(jax.random.uniform(streams_of[3], (NX,), jnp.float32, math.log(0.5), math.log(2.0))), 0.5, 2.0),
        "metric_y": jnp.clip(jnp.exp(jax.random.uniform(streams_of[4], (NY,), jnp.float32, math.log(0.5), math.log(2.0))), 0.5, 2.0),
        "coarse_force": gaussian(streams_of[5], (NYC, NZC, 3, NXC), 1.0, 6.0, ((0, 8), (1, 4))),
        "row_map": draw_row_map(jax.random.fold_in(streams_of[9], 71), 0),
        "x_index": draw_x_index(jax.random.fold_in(streams_of[9], 71), 0),
        "x_weight": jnp.clip(jax.random.uniform(streams_of[8], (NX,), jnp.float32, 0.0, 1.0), 0.0, 1.0).astype(jnp.bfloat16),
    }


rk_weight = 0.5


def refine_levels(extended):
    lower = extended[:, :-1]
    middle = (0.5 * (lower.astype(jnp.float32) + extended[:, 1:].astype(jnp.float32))).astype(jnp.bfloat16)
    stacked = jnp.stack([lower, middle], axis=2)
    return stacked.reshape(extended.shape[0], 2 * (extended.shape[1] - 1), extended.shape[2], extended.shape[3])


def upsample_table(x_index, x_weight, coarse_width):
    positions = jnp.arange(coarse_width, dtype=jnp.int32)[:, None]
    nothing = jnp.zeros((), jnp.bfloat16)
    left_part = jnp.where(positions == x_index[None, :], x_weight[None, :], nothing)
    right_weight = (1.0 - x_weight.astype(jnp.float32)).astype(jnp.bfloat16)
    right_part = jnp.where(positions == x_index[None, :] + 1, right_weight[None, :], nothing)
    return left_part + right_part


def reference(velocity, deriv_x, deriv_y, metric_x, metric_y, coarse_force, row_map, x_index, x_weight):
    table = upsample_table(x_index, x_weight, NXC)
    extended = jnp.concatenate([coarse_force, coarse_force[:, -1:]], axis=1)
    force_levels = refine_levels(extended)
    levels_first = jnp.transpose(force_levels, (1, 0, 2, 3))
    velocity_first = jnp.transpose(velocity, (1, 0, 2, 3))

    def one_level(inputs):
        plane, coarse_plane = inputs
        along_x = jnp.dot(plane.reshape(NY * 3, NX), deriv_x, preferred_element_type=jnp.float32).reshape(NY, 3, NX) * metric_x
        along_y = (jnp.dot(deriv_y, plane.reshape(NY, 3 * NX), preferred_element_type=jnp.float32) * metric_y[:, None]).astype(jnp.bfloat16).reshape(NY, 3, NX)
        chosen = jnp.take(coarse_plane, row_map, axis=0)
        forcing = jnp.dot(chosen.reshape(NY * 3, NXC), table, preferred_element_type=jnp.float32).reshape(NY, 3, NX)
        moving = plane.astype(jnp.float32)
        result = forcing - (moving[:, 0:1] * along_x + moving[:, 1:2] * along_y.astype(jnp.float32))
        return result.astype(jnp.bfloat16), (moving + rk_weight * result).astype(jnp.bfloat16)

    tendency, updated = lax.map(one_level, (velocity_first, levels_first))
    return jnp.transpose(tendency, (1, 0, 2, 3)), jnp.transpose(updated, (1, 0, 2, 3))
```

```python
import functools

import jax
import jax.numpy as jnp
from jax import lax
from jax.experimental import pallas as pl
from jax.experimental.pallas import tpu as pltpu
from jax.sharding import PartitionSpec as P

rk_weight = 0.5
vmem_bytes = 40 * 1024 * 1024
lanes = 128


def refine_levels(extended):
    lower = extended[:, :-1]
    middle = (0.5 * (lower.astype(jnp.float32) + extended[:, 1:].astype(jnp.float32))).astype(
        jnp.bfloat16
    )
    stacked = jnp.stack([lower, middle], axis=2)
    return stacked.reshape(
        extended.shape[0], 2 * (extended.shape[1] - 1), extended.shape[2], extended.shape[3]
    )


def upsample_table(x_index, x_weight, coarse_width):
    positions = jnp.arange(coarse_width, dtype=jnp.int32)[:, None]
    nothing = jnp.zeros((), jnp.bfloat16)
    left_part = jnp.where(positions == x_index[None, :], x_weight[None, :], nothing)
    right_weight = (1.0 - x_weight.astype(jnp.float32)).astype(jnp.bfloat16)
    right_part = jnp.where(positions == x_index[None, :] + 1, right_weight[None, :], nothing)
    return left_part + right_part


def chosen_levels(coarse_force, row_map):
    portion = lax.all_gather(coarse_force, "row", axis=0, tiled=True)
    coarse_rows = portion.shape[0]
    selector = (row_map[:, None] == jnp.arange(coarse_rows, dtype=jnp.int32)[None, :]).astype(
        jnp.bfloat16
    )
    chosen = (
        jnp.dot(selector, portion.reshape(coarse_rows, -1), preferred_element_type=jnp.float32)
        .astype(jnp.bfloat16)
        .reshape((row_map.shape[0],) + coarse_force.shape[1:])
    )
    slabs = lax.axis_size("slab")
    route = [(i + 1, i) for i in range(slabs - 1)]
    upper_rim = lax.ppermute(chosen[:, :1], "slab", route)
    is_topmost = lax.axis_index("slab") == slabs - 1
    rim_level = jnp.where(is_topmost, chosen[:, -1:], upper_rim)
    return refine_levels(jnp.concatenate([chosen, rim_level], axis=1))


def pack_kernel(component, width, v_ref, *refs):
    blocks, sem = refs[:-1], refs[-1]
    z = lax.axis_index("row") // 2
    copies = []
    for s, block in enumerate(blocks, start=1):
        offset = pl.multiple_of((z ^ s) * width, lanes)
        copies.append(
            pltpu.make_async_copy(
                v_ref.at[:, component, :, pl.ds(offset, width)], block, sem.at[s - 1]
            )
        )
    for copy in copies:
        copy.start()
    for copy in copies:
        copy.wait()


def pack(v, component, zs):
    rows, _, levels, fine_width = v.shape
    width = fine_width // zs
    block = jax.ShapeDtypeStruct((rows, levels, width), v.dtype)
    return pl.pallas_call(
        functools.partial(pack_kernel, component, width),
        out_shape=[block] * (zs - 1),
        in_specs=[pl.BlockSpec(memory_space=pl.ANY)],
        out_specs=[pl.BlockSpec(memory_space=pl.ANY)] * (zs - 1),
        scratch_shapes=[pltpu.SemaphoreType.DMA((zs - 1,))],
        cost_estimate=pl.CostEstimate(
            flops=0, bytes_accessed=2 * (zs - 1) * rows * levels * width * 2, transcendentals=0
        ),
        name="pack",
    )(v)


def slope_kernel(xi_ref, d_ref, m_ref, *refs):
    blocks, (send_ref, own_ref, x_all, y_send) = refs[:-4], refs[-4:]
    rows, levels, width = blocks[0].shape
    each = rows * levels
    for s, block in enumerate(blocks):
        x_all[s * each : (s + 1) * each, :] = (
            block[...].astype(jnp.float32).reshape(each, width)
        )
    count = rows * len(blocks)
    columns = jnp.concatenate(
        [x_all[pl.ds(l, count, stride=levels), :] for l in range(levels)], axis=1
    ).astype(jnp.bfloat16)
    slope = jnp.dot(d_ref[...], columns, preferred_element_type=jnp.float32) * m_ref[...]
    for l in range(levels):
        here = slice(l * width, (l + 1) * width)
        y_send[pl.ds(l, count, stride=levels), :] = slope[:count, here]
        own_ref[pl.ds(l, count, stride=levels), :] = slope[count:, here]
    send_ref[...] = y_send[...].reshape(count, levels, width).astype(jnp.bfloat16)


def slopes(v, component, arrived, order, deriv, metric):
    rows, _, levels, fine_width = v.shape
    zs = len(arrived) + 1
    width = fine_width // zs
    count = rows * zs
    steps = width // lanes
    block = pl.BlockSpec((rows, levels, lanes), lambda g, xi: (0, 0, g))
    return pl.pallas_call(
        slope_kernel,
        grid_spec=pltpu.PrefetchScalarGridSpec(
            num_scalar_prefetch=1,
            grid=(steps,),
            in_specs=[
                pl.BlockSpec(deriv.shape, lambda g, xi: (0, 0)),
                pl.BlockSpec(metric.shape, lambda g, xi: (0, 0)),
                pl.BlockSpec(
                    (rows, None, levels, lanes),
                    lambda g, xi: (0, component, 0, xi[0] * steps + g),
                ),
            ]
            + [block] * (zs - 1),
            out_specs=[
                pl.BlockSpec((count, levels, lanes), lambda g, xi: (0, 0, g)),
                pl.BlockSpec((count * levels, lanes), lambda g, xi: (0, g)),
            ],
            scratch_shapes=[
                pltpu.VMEM((count * levels, lanes), jnp.float32),
                pltpu.VMEM((count * levels, lanes), jnp.float32),
            ],
        ),
        out_shape=[
            jax.ShapeDtypeStruct((count, levels, width), jnp.bfloat16),
            jax.ShapeDtypeStruct((count * levels, width), jnp.float32),
        ],
        compiler_params=pltpu.CompilerParams(vmem_limit_bytes=vmem_bytes),
        cost_estimate=pl.CostEstimate(
            flops=4 * count * count * levels * width,
            bytes_accessed=8 * count * levels * width,
            transcendentals=0,
        ),
        name="slopes",
    )(order, deriv, metric, v, *arrived)


def base_kernel(v_ref, v0_ref, d_ref, m_ref, f_ref, t_ref, base_ref):
    rows, levels, width = v_ref.shape
    flat = v_ref[...].astype(jnp.float32).reshape(rows * levels, width).astype(jnp.bfloat16)
    along = jnp.dot(flat, d_ref[...], preferred_element_type=jnp.float32) * m_ref[...]
    force = f_ref[...].astype(jnp.float32).reshape(rows * levels, -1).astype(jnp.bfloat16)
    forcing = jnp.dot(force, t_ref[...], preferred_element_type=jnp.float32)
    carry = v0_ref[...].astype(jnp.float32).reshape(rows * levels, width)
    base_ref[...] = (forcing - carry * along).reshape(rows, levels, width)


def bases(v, component, deriv_x, metric_x, force, table):
    rows, _, levels, width = v.shape
    part = 32
    coarse_width = table.shape[0]
    return pl.pallas_call(
        base_kernel,
        grid=(rows // part,),
        in_specs=[
            pl.BlockSpec((part, None, levels, width), lambda g: (g, component, 0, 0)),
            pl.BlockSpec((part, None, levels, width), lambda g: (g, 0, 0, 0)),
            pl.BlockSpec(deriv_x.shape, lambda g: (0, 0)),
            pl.BlockSpec(metric_x.shape, lambda g: (0, 0)),
            pl.BlockSpec((None, part, levels, coarse_width), lambda g: (component, g, 0, 0)),
            pl.BlockSpec(table.shape, lambda g: (0, 0)),
        ],
        out_specs=pl.BlockSpec((part, levels, width), lambda g: (g, 0, 0)),
        out_shape=jax.ShapeDtypeStruct((rows, levels, width), jnp.float32),
        compiler_params=pltpu.CompilerParams(vmem_limit_bytes=vmem_bytes),
        cost_estimate=pl.CostEstimate(
            flops=2 * rows * levels * width * (width + coarse_width),
            bytes_accessed=8 * rows * levels * width + 2 * width * width,
            transcendentals=0,
        ),
        name="bases",
    )(v, v, deriv_x, metric_x, force, table)


def combine_kernel(xi_ref, base_ref, v_ref, v1_ref, y_ref, *refs):
    t_ref, u_ref = refs[-2:]
    t = base_ref[...] - v1_ref[...].astype(jnp.float32) * y_ref[...].astype(jnp.float32)
    t_ref[...] = t.astype(jnp.bfloat16)
    u_ref[...] = (v_ref[...].astype(jnp.float32) + rk_weight * t).astype(jnp.bfloat16)


def combine(v, component, s, order, base, along_y, outs):
    rows, _, levels, fine_width = v.shape
    width = along_y.shape[2]
    part = 16
    column = lambda c: pl.BlockSpec(
        (part, None, levels, width), lambda g, xi: (g, c, 0, xi[s])
    )
    whole = pl.BlockSpec(memory_space=pl.ANY)
    return pl.pallas_call(
        combine_kernel,
        grid_spec=pltpu.PrefetchScalarGridSpec(
            num_scalar_prefetch=1,
            grid=(rows // part,),
            in_specs=[
                pl.BlockSpec((part, levels, width), lambda g, xi: (g, 0, xi[s])),
                column(component),
                column(1),
                pl.BlockSpec((part, levels, width), lambda g, xi: (g, 0, 0)),
            ]
            + [whole] * len(outs),
            out_specs=[column(component), column(component)],
        ),
        out_shape=[jax.ShapeDtypeStruct(v.shape, v.dtype)] * 2,
        input_output_aliases={5: 0, 6: 1} if outs else {},
        compiler_params=pltpu.CompilerParams(vmem_limit_bytes=vmem_bytes),
        cost_estimate=pl.CostEstimate(
            flops=4 * rows * levels * width,
            bytes_accessed=14 * rows * levels * width,
            transcendentals=0,
        ),
        name="combine",
    )(order, base, v, v, along_y, *outs)


def ring_shards(
    velocity, deriv_x, deriv_y, metric_x, metric_y, coarse_force, row_map, x_index, x_weight
):
    rows, levels, components, fine_width = velocity.shape
    devices = lax.axis_size("row")
    zs = devices // 2
    me = lax.axis_index("row")
    order = ((me // 2) ^ jnp.arange(zs, dtype=jnp.int32)).astype(jnp.int32)
    v = jnp.transpose(velocity, (0, 2, 1, 3))
    partner = lambda s: [(i, i ^ (2 * s)) for i in range(devices)]
    far_first = sorted(range(1, zs), key=lambda s: -s)

    def exchange(blocks):
        moved = {s: lax.ppermute(blocks[s - 1], "row", partner(s)) for s in far_first}
        return [moved[s] for s in range(1, zs)]

    arrived = [exchange(pack(v, c, zs)) for c in range(components)]

    row_order = [me ^ (2 * s + 1) for s in range(zs)] + [me ^ (2 * s) for s in range(zs)]
    piece = lambda a, at, axis: lax.dynamic_slice_in_dim(a, at * rows, rows, axis)
    by_column = jnp.concatenate([piece(deriv_y, me ^ (2 * s), 1) for s in range(zs)], axis=1)
    deriv = jnp.concatenate([piece(by_column, at, 0) for at in row_order], axis=0)
    metric = jnp.concatenate([piece(metric_y, at, 0) for at in row_order], axis=0)[:, None]

    force = jnp.transpose(chosen_levels(coarse_force, row_map), (2, 0, 1, 3))
    table = upsample_table(x_index, x_weight, coarse_force.shape[3])

    outs = ()
    for c in range(components):
        send, own = slopes(v, c, arrived[c], order, deriv, metric)
        got = lax.ppermute(send, "row", [(i, i ^ 1) for i in range(devices)])
        total = (own.reshape(got.shape) + got.astype(jnp.float32)).astype(jnp.bfloat16)
        pieces = [total[s * rows : (s + 1) * rows] for s in range(zs)]
        along_y = pieces[:1] + exchange(pieces[1:])
        base = bases(v, c, deriv_x, metric_x[None, :], force, table)
        for s in [0] + far_first[::-1]:
            outs = combine(v, c, s, order, base, along_y[s], outs)
    tendency, updated = (jnp.transpose(o, (0, 2, 1, 3)) for o in outs)
    return tendency, updated


def general_shards(
    velocity, deriv_x, deriv_y, metric_x, metric_y, coarse_force, row_map, x_index, x_weight
):
    rows, levels, components, fine_width = velocity.shape
    flattened = velocity.reshape(rows, levels * components * fine_width)
    columns = lax.all_to_all(flattened, "row", split_axis=1, concat_axis=0, tiled=True)
    slope_columns = (
        jnp.dot(deriv_y, columns, preferred_element_type=jnp.float32) * metric_y[:, None]
    ).astype(jnp.bfloat16)
    along_y = lax.all_to_all(slope_columns, "row", split_axis=0, concat_axis=1, tiled=True).reshape(
        velocity.shape
    )
    along_x = (
        jnp.dot(
            velocity.reshape(-1, fine_width), deriv_x, preferred_element_type=jnp.float32
        ).reshape(velocity.shape)
        * metric_x
    )
    coarse_width = coarse_force.shape[3]
    force = chosen_levels(coarse_force, row_map)
    table = upsample_table(x_index, x_weight, coarse_width)
    forcing = jnp.dot(
        force.reshape(-1, coarse_width), table, preferred_element_type=jnp.float32
    ).reshape(velocity.shape)
    moving = velocity.astype(jnp.float32)
    result = forcing - (
        moving[:, :, 0:1] * along_x + moving[:, :, 1:2] * along_y.astype(jnp.float32)
    )
    return (result.astype(jnp.bfloat16), (moving + rk_weight * result).astype(jnp.bfloat16))


def solution(mesh):
    shards = ring_shards if mesh.shape["row"] == 8 else general_shards
    return jax.shard_map(
        shards,
        mesh=mesh,
        in_specs=(
            P("row", "slab", None, None),
            P(),
            P(),
            P(),
            P(),
            P("row", "slab", None, None),
            P("row"),
            P(),
            P(),
        ),
        out_specs=(P("row", "slab", None, None), P("row", "slab", None, None)),
        check_vma=False,
    )
```

```python
import functools

import jax
import jax.numpy as jnp
from jax import lax
from jax.experimental import pallas as pl
from jax.experimental.pallas import tpu as pltpu
from jax.sharding import PartitionSpec as P

rk_weight = 0.5
mib = 1024 * 1024
lanes = 128
in_flight = 5
light = pl.CostEstimate(flops=1, bytes_accessed=1, transcendentals=0)


def refine_levels(extended):
    lower = extended[:, :-1]
    middle = (0.5 * (lower.astype(jnp.float32) + extended[:, 1:].astype(jnp.float32))).astype(
        jnp.bfloat16
    )
    stacked = jnp.stack([lower, middle], axis=2)
    return stacked.reshape(
        extended.shape[0], 2 * (extended.shape[1] - 1), extended.shape[2], extended.shape[3]
    )


def upsample_table(x_index, x_weight, coarse_width):
    positions = jnp.arange(coarse_width, dtype=jnp.int32)[:, None]
    nothing = jnp.zeros((), jnp.bfloat16)
    left_part = jnp.where(positions == x_index[None, :], x_weight[None, :], nothing)
    right_weight = (1.0 - x_weight.astype(jnp.float32)).astype(jnp.bfloat16)
    right_part = jnp.where(positions == x_index[None, :] + 1, right_weight[None, :], nothing)
    return left_part + right_part


def chosen_levels(portion, coarse_rows, row_map):
    selector = (row_map[:, None] == coarse_rows[None, :]).astype(jnp.bfloat16)
    chosen = (
        jnp.dot(
            selector, portion.reshape(portion.shape[0], -1), preferred_element_type=jnp.float32
        )
        .astype(jnp.bfloat16)
        .reshape((row_map.shape[0],) + portion.shape[1:])
    )
    return extended_levels(chosen)


def extended_levels(chosen):
    slabs = lax.axis_size("slab")
    route = [(i + 1, i) for i in range(slabs - 1)]
    upper_rim = lax.ppermute(chosen[:, :1], "slab", route)
    is_topmost = lax.axis_index("slab") == slabs - 1
    rim_level = jnp.where(is_topmost, chosen[:, -1:], upper_rim)
    return refine_levels(jnp.concatenate([chosen, rim_level], axis=1))


def pack_kernel(xi_ref, v_ref, *refs):
    blocks, wide = refs[:-1], refs[-1]
    rows, comps, levels, width = v_ref.shape
    half = levels // 2
    for c in range(comps):
        for j in range(width // lanes):
            lane = slice(j * lanes, (j + 1) * lanes)
            wide[...] = v_ref[:, c, :, lane].astype(jnp.float32).reshape(rows * levels, lanes)
            for i, block in enumerate(blocks):
                start = (xi_ref[0] ^ i) * half
                for l in range(half):
                    level = wide[pl.ds(start + l, rows, stride=levels), :]
                    block[c * half + l, :, lane] = level.astype(block.dtype)


def pack(v, comps, s, prefetch):
    rows, _, levels, fine_width = v.shape
    zs = prefetch.shape[0] - 1
    width = fine_width // zs
    planes = len(comps) * levels // 2
    part = rows // 2
    block = jax.ShapeDtypeStruct((2 * planes, part, width), v.dtype)
    return pl.pallas_call(
        pack_kernel,
        grid_spec=pltpu.PrefetchScalarGridSpec(
            num_scalar_prefetch=1,
            grid=(2,),
            in_specs=[
                pl.BlockSpec(
                    (part, len(comps), levels, width),
                    lambda g, xi: (g, comps[0] // len(comps), 0, xi[1 + s]),
                )
            ],
            out_specs=[pl.BlockSpec((planes, part, width), lambda g, xi: (g, 0, 0))] * 2,
            scratch_shapes=[pltpu.VMEM((part * levels, lanes), jnp.float32)],
        ),
        out_shape=[block] * 2,
        compiler_params=pltpu.CompilerParams(vmem_limit_bytes=60 * mib),
        cost_estimate=light,
        name="pack",
    )(prefetch, v)


def slope_kernel(planes, d_ref, m_ref, *refs):
    count = len(refs) // 2
    sources, results = refs[:count], refs[count:]
    part, width = sources[0].shape[1:]
    for q in range(planes):
        columns = jnp.concatenate(
            [source[h * planes + q] for source in sources for h in range(2)], axis=0
        )
        slope = jnp.dot(d_ref[...], columns, preferred_element_type=jnp.float32) * m_ref[...]
        slope = slope.astype(jnp.bfloat16)
        for k, result in enumerate(results):
            for h in range(2):
                at = (2 * k + h) * part
                result[h * planes + q] = slope[at : at + part]


def slopes(blocks, planes, deriv, metric):
    part, width = blocks[0].shape[1:]
    count = len(blocks)
    result = jax.ShapeDtypeStruct((2 * planes, part, width), jnp.bfloat16)
    area = deriv.shape[0] * planes * width
    return pl.pallas_call(
        functools.partial(slope_kernel, planes),
        in_specs=[pl.BlockSpec(memory_space=pltpu.VMEM)] * (2 + count),
        out_specs=[pl.BlockSpec(memory_space=pltpu.VMEM)] * count,
        out_shape=[result] * count,
        compiler_params=pltpu.CompilerParams(vmem_limit_bytes=32 * mib),
        cost_estimate=light,
        name="slopes",
    )(deriv, metric, *blocks)


def hold_kernel(block_ref, *refs):
    refs[-1][...] = block_ref[...]


def hold(block, after):
    return pl.pallas_call(
        hold_kernel,
        in_specs=[pl.BlockSpec(memory_space=pltpu.VMEM)]
        + [pl.BlockSpec(memory_space=pl.ANY)] * len(after),
        out_specs=pl.BlockSpec(memory_space=pltpu.VMEM),
        out_shape=jax.ShapeDtypeStruct(block.shape, block.dtype),
        compiler_params=pltpu.CompilerParams(vmem_limit_bytes=8 * mib),
        cost_estimate=light,
        name="hold",
    )(block, *after)


def base_kernel(v_ref, v0_ref, d_ref, m_ref, f_ref, t_ref, base_ref):
    rows, levels, width = v_ref.shape
    flat = v_ref[...].astype(jnp.float32).reshape(rows * levels, width).astype(jnp.bfloat16)
    along = jnp.dot(flat, d_ref[...], preferred_element_type=jnp.float32) * m_ref[...]
    force = f_ref[...].astype(jnp.float32).reshape(rows * levels, -1).astype(jnp.bfloat16)
    forcing = jnp.dot(force, t_ref[...], preferred_element_type=jnp.float32)
    carry = v0_ref[...].astype(jnp.float32).reshape(rows * levels, width)
    base_ref[...] = (forcing - carry * along).reshape(rows, levels, width)


def bases(v, component, deriv_x, metric_x, force, table):
    rows, _, levels, width = v.shape
    part = 32
    coarse_width = table.shape[0]
    return pl.pallas_call(
        base_kernel,
        grid=(rows // part,),
        in_specs=[
            pl.BlockSpec((part, None, levels, width), lambda g: (g, component, 0, 0)),
            pl.BlockSpec((part, None, levels, width), lambda g: (g, 0, 0, 0)),
            pl.BlockSpec(deriv_x.shape, lambda g: (0, 0)),
            pl.BlockSpec(metric_x.shape, lambda g: (0, 0)),
            pl.BlockSpec((None, part, levels, coarse_width), lambda g: (component, g, 0, 0)),
            pl.BlockSpec(table.shape, lambda g: (0, 0)),
        ],
        out_specs=pl.BlockSpec((part, levels, width), lambda g: (g, 0, 0)),
        out_shape=jax.ShapeDtypeStruct((rows, levels, width), jnp.float32),
        compiler_params=pltpu.CompilerParams(vmem_limit_bytes=32 * mib),
        cost_estimate=light,
        name="bases",
    )(v, v, deriv_x, metric_x, force, table)


def combine_kernel(xi_ref, base_ref, v_ref, v1_ref, near_ref, far_ref, *refs):
    t_ref, u_ref, along = refs[-3:]
    rows, levels, width = base_ref.shape
    half = levels // 2
    for j in range(width // lanes):
        lane = slice(j * lanes, (j + 1) * lanes)
        for i, block in enumerate((near_ref, far_ref)):
            start = (xi_ref[0] ^ i) * half
            for l in range(half):
                plane = block[l, :, lane].astype(jnp.float32)
                along[pl.ds(start + l, rows, stride=levels), :] = plane
        along_y = along[...].reshape(rows, levels, lanes)
        t = base_ref[:, :, lane] - v1_ref[:, :, lane].astype(jnp.float32) * along_y
        t_ref[:, :, lane] = t.astype(jnp.bfloat16)
        moved = v_ref[:, :, lane].astype(jnp.float32) + rk_weight * t
        u_ref[:, :, lane] = moved.astype(jnp.bfloat16)


def combine(v, component, at, s, prefetch, base, near, far, outs):
    rows, _, levels, fine_width = v.shape
    part, width = near.shape[1:]
    half = levels // 2
    per_half = near.shape[0] // 2 // half
    column = lambda c: pl.BlockSpec(
        (part, None, levels, width), lambda g, xi: (g, c, 0, xi[1 + s])
    )
    planes = pl.BlockSpec((half, part, width), lambda g, xi: (g * per_half + at, 0, 0))
    return pl.pallas_call(
        combine_kernel,
        grid_spec=pltpu.PrefetchScalarGridSpec(
            num_scalar_prefetch=1,
            grid=(rows // part,),
            in_specs=[
                pl.BlockSpec((part, levels, width), lambda g, xi: (g, 0, xi[1 + s])),
                column(component),
                column(1),
                planes,
                planes,
            ]
            + [pl.BlockSpec(memory_space=pl.ANY)] * len(outs),
            out_specs=[column(component), column(component)],
            scratch_shapes=[pltpu.VMEM((part * levels, lanes), jnp.float32)],
        ),
        out_shape=[jax.ShapeDtypeStruct(v.shape, v.dtype)] * 2,
        input_output_aliases={6: 0, 7: 1} if outs else {},
        compiler_params=pltpu.CompilerParams(vmem_limit_bytes=16 * mib),
        cost_estimate=light,
        name="combine",
    )(prefetch, base, v, v, near, far, *outs)


def ring_shards(
    velocity, deriv_x, deriv_y, metric_x, metric_y, coarse_force, row_map, x_index, x_weight
):
    rows, levels, components, fine_width = velocity.shape
    devices = lax.axis_size("row")
    zs = devices // 2
    me = lax.axis_index("row").astype(jnp.int32)
    prefetch = jnp.concatenate([(me % 2)[None], (me // 2) ^ jnp.arange(zs, dtype=jnp.int32)])
    v = jnp.transpose(velocity, (0, 2, 1, 3))
    arrival = [0, 4, 2, 5, 6, 3, 7, 1]
    place = {k: at for at, k in enumerate(arrival)}
    moved = []

    def trade(block, k):
        if len(moved) >= in_flight:
            block, moved[-in_flight] = lax.optimization_barrier((block, moved[-in_flight]))
        moved.append(lax.ppermute(block, "row", [(i, i ^ k) for i in range(devices)]))
        return moved[-1]

    def exchange(blocks):
        here = [blocks[0]]
        for k, block in zip(arrival[1:], blocks[1:]):
            here.append(trade(block, k))
        return here

    coarse_here, coarse_levels, _, coarse_width = coarse_force.shape
    row_size = coarse_levels * components * coarse_width
    coarse = jnp.transpose(coarse_force, (0, 2, 1, 3))
    portion = jnp.concatenate([coarse, trade(coarse, 4)], axis=0)

    chunks = [(0, 1), (2,)]
    arrived = []
    for comps in chunks:
        blocks = {}
        for s in (2, 1, 3, 0):
            blocks[2 * s], blocks[2 * s + 1] = pack(v, comps, s, prefetch)
        arrived.append(exchange([blocks[k] for k in arrival]))
        k = 2 if len(arrived) == 1 else 1
        portion = jnp.concatenate([portion, trade(portion, k)], axis=0)

    partners = [me ^ k for k in arrival]
    piece = lambda a, at, axis: lax.dynamic_slice_in_dim(a, at * rows, rows, axis)
    by_column = jnp.concatenate([piece(deriv_y, at, 1) for at in partners], axis=1)
    deriv = jnp.concatenate([piece(by_column, at, 0) for at in partners], axis=0)
    metric = jnp.concatenate([piece(metric_y, at, 0) for at in partners], axis=0)[:, None]

    holders = jnp.stack([me ^ k for k in (0, 4, 2, 6, 1, 5, 3, 7)])
    coarse_rows = (
        holders[:, None] * coarse_here + jnp.arange(coarse_here, dtype=jnp.int32)
    ).reshape(-1)
    portion = portion.reshape(-1, row_size)
    selector = (row_map[:, None] == coarse_rows[None, :]).astype(jnp.bfloat16)
    chosen = jnp.dot(selector, portion, preferred_element_type=jnp.float32).astype(jnp.bfloat16)
    chosen = chosen.reshape(rows, components, coarse_levels, coarse_width)
    force = jnp.transpose(
        extended_levels(jnp.transpose(chosen, (0, 2, 1, 3))), (2, 0, 1, 3)
    )
    table = upsample_table(x_index, x_weight, coarse_width)

    base = [
        bases(v, c, deriv_x, metric_x[None, :], force, table) for c in range(components)
    ]
    outs = ()
    for comps, blocks in zip(chunks, arrived):
        sent = list(slopes(blocks, len(comps) * levels // 2, deriv, metric))
        if outs:
            sent[-1] = hold(sent[-1], (*outs, base[comps[0]]))
        along_y = exchange(sent)
        for at, c in enumerate(comps):
            for s in (2, 3, 1, 0):
                near, far = along_y[place[2 * s]], along_y[place[2 * s + 1]]
                outs = combine(v, c, at, s, prefetch, base[c], near, far, outs)
    tendency, updated = (jnp.transpose(o, (0, 2, 1, 3)) for o in outs)
    return tendency, updated


def general_shards(
    velocity, deriv_x, deriv_y, metric_x, metric_y, coarse_force, row_map, x_index, x_weight
):
    rows, levels, components, fine_width = velocity.shape
    flattened = velocity.reshape(rows, levels * components * fine_width)
    columns = lax.all_to_all(flattened, "row", split_axis=1, concat_axis=0, tiled=True)
    slope_columns = (
        jnp.dot(deriv_y, columns, preferred_element_type=jnp.float32) * metric_y[:, None]
    ).astype(jnp.bfloat16)
    along_y = lax.all_to_all(slope_columns, "row", split_axis=0, concat_axis=1, tiled=True).reshape(
        velocity.shape
    )
    along_x = (
        jnp.dot(
            velocity.reshape(-1, fine_width), deriv_x, preferred_element_type=jnp.float32
        ).reshape(velocity.shape)
        * metric_x
    )
    coarse_width = coarse_force.shape[3]
    portion = lax.all_gather(coarse_force, "row", axis=0, tiled=True)
    force = chosen_levels(portion, jnp.arange(portion.shape[0], dtype=jnp.int32), row_map)
    table = upsample_table(x_index, x_weight, coarse_width)
    forcing = jnp.dot(
        force.reshape(-1, coarse_width), table, preferred_element_type=jnp.float32
    ).reshape(velocity.shape)
    moving = velocity.astype(jnp.float32)
    result = forcing - (
        moving[:, :, 0:1] * along_x + moving[:, :, 1:2] * along_y.astype(jnp.float32)
    )
    return (result.astype(jnp.bfloat16), (moving + rk_weight * result).astype(jnp.bfloat16))


def solution(mesh):
    shards = ring_shards if mesh.shape["row"] == 8 else general_shards
    return jax.shard_map(
        shards,
        mesh=mesh,
        in_specs=(
            P("row", "slab", None, None),
            P(),
            P(),
            P(),
            P(),
            P("row", "slab", None, None),
            P("row"),
            P(),
            P(),
        ),
        out_specs=(P("row", "slab", None, None), P("row", "slab", None, None)),
        check_vma=False,
    )
```

```python
import functools

import jax
import jax.numpy as jnp
from jax import lax
from jax.experimental import pallas as pl
from jax.experimental.pallas import tpu as pltpu
from jax.sharding import PartitionSpec as P

rk_weight = 0.5
mib = 1024 * 1024
lanes = 128
in_flight = 5
light = pl.CostEstimate(flops=1, bytes_accessed=1, transcendentals=0)


def refine_levels(extended):
    lower = extended[:, :-1]
    middle = (0.5 * (lower.astype(jnp.float32) + extended[:, 1:].astype(jnp.float32))).astype(
        jnp.bfloat16
    )
    stacked = jnp.stack([lower, middle], axis=2)
    return stacked.reshape(
        extended.shape[0], 2 * (extended.shape[1] - 1), extended.shape[2], extended.shape[3]
    )


def upsample_table(x_index, x_weight, coarse_width):
    positions = jnp.arange(coarse_width, dtype=jnp.int32)[:, None]
    nothing = jnp.zeros((), jnp.bfloat16)
    left_part = jnp.where(positions == x_index[None, :], x_weight[None, :], nothing)
    right_weight = (1.0 - x_weight.astype(jnp.float32)).astype(jnp.bfloat16)
    right_part = jnp.where(positions == x_index[None, :] + 1, right_weight[None, :], nothing)
    return left_part + right_part


def chosen_levels(portion, coarse_rows, row_map):
    selector = (row_map[:, None] == coarse_rows[None, :]).astype(jnp.bfloat16)
    chosen = (
        jnp.dot(
            selector, portion.reshape(portion.shape[0], -1), preferred_element_type=jnp.float32
        )
        .astype(jnp.bfloat16)
        .reshape((row_map.shape[0],) + portion.shape[1:])
    )
    return extended_levels(chosen)


def extended_levels(chosen):
    slabs = lax.axis_size("slab")
    route = [(i + 1, i) for i in range(slabs - 1)]
    upper_rim = lax.ppermute(chosen[:, :1], "slab", route)
    is_topmost = lax.axis_index("slab") == slabs - 1
    rim_level = jnp.where(is_topmost, chosen[:, -1:], upper_rim)
    return refine_levels(jnp.concatenate([chosen, rim_level], axis=1))


def pack_kernel(xi_ref, v_ref, *refs):
    blocks, wide = refs[-3:-1], refs[-1]
    rows, comps, levels, width = v_ref.shape
    half = levels // 2
    for c in range(comps):
        for j in range(width // lanes):
            lane = slice(j * lanes, (j + 1) * lanes)
            wide[...] = v_ref[:, c, :, lane].astype(jnp.float32).reshape(rows * levels, lanes)
            for i, block in enumerate(blocks):
                start = (xi_ref[0] ^ i) * half
                for l in range(half):
                    level = wide[pl.ds(start + l, rows, stride=levels), :]
                    block[c * half + l, :, lane] = level.astype(block.dtype)


def pack(v, comps, s, prefetch, after):
    rows, _, levels, fine_width = v.shape
    zs = prefetch.shape[0] - 1
    width = fine_width // zs
    planes = len(comps) * levels // 2
    part = rows // 2
    block = jax.ShapeDtypeStruct((2 * planes, part, width), v.dtype)
    return pl.pallas_call(
        pack_kernel,
        grid_spec=pltpu.PrefetchScalarGridSpec(
            num_scalar_prefetch=1,
            grid=(2,),
            in_specs=[
                pl.BlockSpec(
                    (part, len(comps), levels, width),
                    lambda g, xi: (g, comps[0] // len(comps), 0, xi[1 + s]),
                )
            ]
            + [pl.BlockSpec(memory_space=pl.ANY)] * len(after),
            out_specs=[pl.BlockSpec((planes, part, width), lambda g, xi: (g, 0, 0))] * 2,
            scratch_shapes=[pltpu.VMEM((part * levels, lanes), jnp.float32)],
        ),
        out_shape=[block] * 2,
        compiler_params=pltpu.CompilerParams(vmem_limit_bytes=60 * mib),
        cost_estimate=light,
        name="pack",
    )(prefetch, v, *after)


def slope_kernel(planes, places, riders, d_ref, m_ref, *refs):
    count = len(places)
    sources, results = refs[:count], refs[-count:]
    part, width = sources[0].shape[1:]
    for q in range(planes):
        columns = jnp.concatenate(
            [
                source[h * stride + start + q]
                for source, (stride, start) in zip(sources, places)
                for h in range(2)
            ],
            axis=0,
        )
        slope = jnp.dot(d_ref[...], columns, preferred_element_type=jnp.float32) * m_ref[...]
        slope = slope.astype(jnp.bfloat16)
        for k, result in enumerate(results):
            for h in range(2):
                at = (2 * k + h) * part
                result[h * planes + q] = slope[at : at + part]
    for at in riders:
        results[at][2 * planes :] = refs[count][...]


def slopes(blocks, places, planes, deriv, metric, rider=None, riders=()):
    part, width = blocks[0].shape[1:]
    count = len(blocks)
    more = [rider] if riders else []
    extra = [rider.shape[0] if at in riders else 0 for at in range(count)]
    return pl.pallas_call(
        functools.partial(slope_kernel, planes, places, riders),
        in_specs=[pl.BlockSpec(memory_space=pltpu.VMEM)] * (2 + count + len(more)),
        out_specs=[pl.BlockSpec(memory_space=pltpu.VMEM)] * count,
        out_shape=[
            jax.ShapeDtypeStruct((2 * planes + e, part, width), jnp.bfloat16) for e in extra
        ],
        compiler_params=pltpu.CompilerParams(vmem_limit_bytes=60 * mib),
        cost_estimate=light,
        name="slopes",
    )(deriv, metric, *blocks, *more)


def hold_kernel(block_ref, *refs):
    refs[-1][...] = block_ref[...]


def hold(block, after):
    return pl.pallas_call(
        hold_kernel,
        in_specs=[pl.BlockSpec(memory_space=pltpu.VMEM)]
        + [pl.BlockSpec(memory_space=pl.ANY)] * len(after),
        out_specs=pl.BlockSpec(memory_space=pltpu.VMEM),
        out_shape=jax.ShapeDtypeStruct(block.shape, block.dtype),
        compiler_params=pltpu.CompilerParams(vmem_limit_bytes=8 * mib),
        cost_estimate=light,
        name="hold",
    )(block, *after)


def choose_kernel(pick_ref, spread_ref, rider_ref, *refs):
    blocks, (levels_ref, rim_ref) = refs[:-2], refs[-2:]
    planes, part, width = rider_ref.shape
    rows = levels_ref.shape[1]
    parts = [rider_ref[...]] + [block[block.shape[0] - planes :] for block in blocks]
    source = jnp.concatenate(
        [p.astype(jnp.float32).reshape(planes * part, width) for p in parts], axis=0
    ).astype(jnp.bfloat16)
    chosen = jnp.dot(pick_ref[...], source, preferred_element_type=jnp.float32)
    chosen = chosen.astype(jnp.bfloat16)
    count = spread_ref.shape[0]
    pieces = pick_ref.shape[0] // rows
    for u in range(pieces):
        for h in range(count):
            level = jnp.dot(
                chosen[u * rows : (u + 1) * rows],
                spread_ref[h],
                preferred_element_type=jnp.float32,
            ).astype(jnp.bfloat16)
            levels_ref[u * count + h] = level
            if h == 0 and u % (pieces // rim_ref.shape[0]) == 0:
                rim_ref[u // (pieces // rim_ref.shape[0])] = level


def choose(pick, spread, rider, blocks, components):
    count, _, wide = spread.shape
    rows = 2 * rider.shape[1]
    pieces = pick.shape[0] // rows
    whole = pl.BlockSpec(memory_space=pltpu.VMEM)
    return pl.pallas_call(
        choose_kernel,
        in_specs=[whole] * (3 + len(blocks)),
        out_specs=[whole] * 2,
        out_shape=[
            jax.ShapeDtypeStruct((pieces * count, rows, wide), jnp.bfloat16),
            jax.ShapeDtypeStruct((components, rows, wide), jnp.bfloat16),
        ],
        compiler_params=pltpu.CompilerParams(vmem_limit_bytes=32 * mib),
        cost_estimate=light,
        name="choose",
    )(pick, spread, rider, *blocks)


def refine_kernel(top_ref, levels_ref, rim_ref, force_ref, wide):
    components, rows, fine, width = force_ref.shape
    coarse = fine // 2
    for c in range(components):
        level = [levels_ref[c * coarse + m].astype(jnp.float32) for m in range(coarse)]
        above = rim_ref[c].astype(jnp.float32)
        level.append(jnp.where(top_ref[0] == 1, level[-1], above))
        for j in range(width // lanes):
            lane = slice(j * lanes, (j + 1) * lanes)
            for m in range(coarse):
                low, high = level[m][:, lane], level[m + 1][:, lane]
                wide[pl.ds(2 * m, rows, stride=fine), :] = low
                middle = (0.5 * (low + high)).astype(jnp.bfloat16).astype(jnp.float32)
                wide[pl.ds(2 * m + 1, rows, stride=fine), :] = middle
            force_ref[c, :, :, lane] = (
                wide[...].reshape(rows, fine, lanes).astype(jnp.bfloat16)
            )


def refine(levels, rim, is_topmost):
    components, rows, width = rim.shape
    fine = 2 * levels.shape[0] // components
    whole = pl.BlockSpec(memory_space=pltpu.VMEM)
    return pl.pallas_call(
        refine_kernel,
        in_specs=[pl.BlockSpec(memory_space=pltpu.SMEM), whole, whole],
        out_specs=whole,
        out_shape=jax.ShapeDtypeStruct((components, rows, fine, width), jnp.bfloat16),
        scratch_shapes=[pltpu.VMEM((rows * fine, lanes), jnp.float32)],
        compiler_params=pltpu.CompilerParams(vmem_limit_bytes=32 * mib),
        cost_estimate=light,
        name="refine",
    )(is_topmost.astype(jnp.int32)[None], levels, rim)


def base_kernel(v_ref, v0_ref, d_ref, m_ref, f_ref, t_ref, base_ref):
    rows, levels, width = v_ref.shape
    flat = v_ref[...].astype(jnp.float32).reshape(rows * levels, width).astype(jnp.bfloat16)
    along = jnp.dot(flat, d_ref[...], preferred_element_type=jnp.float32) * m_ref[...]
    force = f_ref[...].astype(jnp.float32).reshape(rows * levels, -1).astype(jnp.bfloat16)
    forcing = jnp.dot(force, t_ref[...], preferred_element_type=jnp.float32)
    carry = v0_ref[...].astype(jnp.float32).reshape(rows * levels, width)
    base_ref[...] = (forcing - carry * along).reshape(rows, levels, width)


def bases(v, comps, deriv_x, metric_x, force, table):
    rows, _, levels, width = v.shape
    part = 32
    coarse_width = table.shape[0]
    first = comps[0]
    return pl.pallas_call(
        base_kernel,
        grid=(rows // part, len(comps)),
        in_specs=[
            pl.BlockSpec((part, None, levels, width), lambda g, c: (g, first + c, 0, 0)),
            pl.BlockSpec((part, None, levels, width), lambda g, c: (g, 0, 0, 0)),
            pl.BlockSpec(deriv_x.shape, lambda g, c: (0, 0)),
            pl.BlockSpec(metric_x.shape, lambda g, c: (0, 0)),
            pl.BlockSpec((None, part, levels, coarse_width), lambda g, c: (first + c, g, 0, 0)),
            pl.BlockSpec(table.shape, lambda g, c: (0, 0)),
        ],
        out_specs=pl.BlockSpec((part, None, levels, width), lambda g, c: (g, c, 0, 0)),
        out_shape=jax.ShapeDtypeStruct((rows, len(comps), levels, width), jnp.float32),
        compiler_params=pltpu.CompilerParams(vmem_limit_bytes=32 * mib),
        cost_estimate=light,
        name="bases",
    )(v, v, deriv_x, metric_x, force, table)


def combine_kernel(xi_ref, base_ref, v_ref, v1_ref, near_ref, far_ref, *refs):
    t_ref, u_ref, mark_ref, along = refs[-4:]
    mark_ref[...] = jnp.zeros(mark_ref.shape, mark_ref.dtype)
    rows, levels, width = base_ref.shape
    half = levels // 2
    for j in range(width // lanes):
        lane = slice(j * lanes, (j + 1) * lanes)
        for i, block in enumerate((near_ref, far_ref)):
            start = (xi_ref[0] ^ i) * half
            for l in range(half):
                plane = block[l, :, lane].astype(jnp.float32)
                along[pl.ds(start + l, rows, stride=levels), :] = plane
        along_y = along[...].reshape(rows, levels, lanes)
        t = base_ref[:, :, lane] - v1_ref[:, :, lane].astype(jnp.float32) * along_y
        t_ref[:, :, lane] = t.astype(jnp.bfloat16)
        moved = v_ref[:, :, lane].astype(jnp.float32) + rk_weight * t
        u_ref[:, :, lane] = moved.astype(jnp.bfloat16)


def combine(v, comps, s, prefetch, base, near, far, outs, after):
    rows, _, levels, fine_width = v.shape
    part, width = near.shape[1:]
    half = levels // 2
    first, count = comps[0], len(comps)
    block = (part, None, levels, width)
    column = pl.BlockSpec(block, lambda g, c, xi: (g, first + c, 0, xi[1 + s]))
    planes = pl.BlockSpec((half, part, width), lambda g, c, xi: (g * count + c, 0, 0))
    return pl.pallas_call(
        combine_kernel,
        grid_spec=pltpu.PrefetchScalarGridSpec(
            num_scalar_prefetch=1,
            grid=(rows // part, count),
            in_specs=[
                pl.BlockSpec(block, lambda g, c, xi: (g, c, 0, xi[1 + s])),
                column,
                pl.BlockSpec(block, lambda g, c, xi: (g, 1, 0, xi[1 + s])),
                planes,
                planes,
            ]
            + [pl.BlockSpec(memory_space=pl.ANY)] * len((*outs[:2], *after)),
            out_specs=[column, column, pl.BlockSpec((8, lanes), lambda g, c, xi: (0, 0))],
            scratch_shapes=[pltpu.VMEM((part * levels, lanes), jnp.float32)],
        ),
        out_shape=[jax.ShapeDtypeStruct(v.shape, v.dtype)] * 2
        + [jax.ShapeDtypeStruct((8, lanes), jnp.float32)],
        input_output_aliases={6: 0, 7: 1} if outs else {},
        compiler_params=pltpu.CompilerParams(vmem_limit_bytes=16 * mib),
        cost_estimate=light,
        name="combine",
    )(prefetch, base, v, v, near, far, *outs[:2], *after)


def ring_shards(
    velocity, deriv_x, deriv_y, metric_x, metric_y, coarse_force, row_map, x_index, x_weight
):
    rows, levels, components, fine_width = velocity.shape
    devices = lax.axis_size("row")
    zs = devices // 2
    width = fine_width // zs
    me = lax.axis_index("row").astype(jnp.int32)
    prefetch = jnp.concatenate([(me % 2)[None], (me // 2) ^ jnp.arange(zs, dtype=jnp.int32)])
    v = jnp.transpose(velocity, (0, 2, 1, 3))
    arrival = [0, 4, 5, 6, 7, 2, 3, 1]
    place = {k: at for at, k in enumerate(arrival)}
    moved, ready = [], []

    def trade(block, k):
        if ready:
            block, ready[-1] = lax.optimization_barrier((block, ready[-1]))
        if len(moved) >= in_flight:
            block, moved[-in_flight] = lax.optimization_barrier((block, moved[-in_flight]))
        ready.append(block)
        at = len(moved)
        moved.append(lax.ppermute(block, "row", [(i, i ^ k) for i in range(devices)]))
        return at

    coarse_here, coarse_levels, _, coarse_width = coarse_force.shape
    row_size = coarse_levels * components * coarse_width
    every = tuple(range(components))
    chunks = one, two = [every[2:], every[:2]]
    blocks, after = {}, ()
    for which, s in ((one, 2), (every, 1), (one, 3), (every, 0), (two, 2), (two, 3)):
        pair = pack(v, which, s, prefetch, after)
        blocks[which, 2 * s], blocks[which, 2 * s + 1] = pair
        after = pair[:1]
    landed = {(every, 0): blocks[every, 0]}
    rider = (
        jnp.transpose(coarse_force, (0, 2, 1, 3))
        .reshape(coarse_here, row_size)
        .reshape(-1, rows // 2, width)
    )
    blocks[one, 4] = jnp.concatenate([blocks[one, 4], rider], axis=0)
    steps = [
        (one, 5), (one, 4), (one, 6), (every, 2), (one, 7), (every, 3), (two, 4), (every, 1),
        (two, 5), (two, 6), (two, 7),
    ]
    partners = [me ^ k for k in arrival]
    piece = lambda a, at, axis: lax.dynamic_slice_in_dim(a, at * rows, rows, axis)
    by_column = jnp.concatenate([piece(deriv_y, at, 1) for at in partners], axis=1)
    deriv = jnp.concatenate([piece(by_column, at, 0) for at in partners], axis=0)
    metric = jnp.concatenate([piece(metric_y, at, 0) for at in partners], axis=0)[:, None]
    numbers = {}

    for step in steps:
        block = blocks[step]
        if step == (every, 2):
            block, deriv, metric = lax.optimization_barrier((block, deriv, metric))
        numbers[step] = trade(block, step[1])
    rider = jnp.concatenate([rider, moved[numbers[one, 4]][-rider.shape[0] :]], axis=0)

    def derivatives(chunk, *carried):
        names = [(every if k < 4 else chunk, k) for k in arrival]
        blocks = [landed[n] if n in landed else moved[numbers[n]] for n in names]
        half = levels // 2
        places = [
            (len(every) * half, chunk[0] * half) if k < 4 else (len(chunk) * half, 0)
            for k in arrival
        ]
        return slopes(blocks, places, len(chunk) * half, deriv, metric, *carried)

    sent = {0: derivatives(one, rider, [place[k] for k in (2, 3, 1)])}
    sent[1] = derivatives(two)
    back = {0: {0: sent[0][0]}, 1: {0: sent[1][0]}}
    for at, k in ((0, 5), (0, 4), (0, 2), (0, 6), (0, 3), (0, 1), (0, 7), (1, 4), (1, 5)):
        back[at][k] = trade(sent[at][place[k]], k)

    holders = jnp.stack([me ^ k for k in (0, 4, 2, 6, 3, 7, 1, 5)])
    pieces = row_size // width
    held = coarse_here * pieces
    names = (holders[:, None] * held + jnp.arange(held, dtype=jnp.int32)).reshape(-1)
    wanted = row_map[None, :] * pieces + jnp.arange(pieces, dtype=jnp.int32)[:, None]
    pick = (wanted.reshape(-1, 1) == names[None, :]).astype(jnp.bfloat16)
    side = width // coarse_width
    wide = -(-coarse_width // lanes) * lanes
    column = jnp.arange(wide, dtype=jnp.int32)
    source = jnp.arange(side, dtype=jnp.int32)[:, None] * coarse_width + column
    source = jnp.where(column < coarse_width, source, -1)
    spread = (
        jnp.arange(width, dtype=jnp.int32)[None, :, None] == source[:, None, :]
    ).astype(jnp.bfloat16)
    carriers = [moved[back[0][k]] for k in (2, 3, 1)]
    chosen, lowest = choose(pick, spread, rider, carriers, components)
    slabs = lax.axis_size("slab")
    rim = lax.ppermute(lowest, "slab", [(i + 1, i) for i in range(slabs - 1)])
    force = refine(chosen, rim, lax.axis_index("slab") == slabs - 1)
    table = upsample_table(x_index, x_weight, wide)
    base = [bases(v, c, deriv_x, metric_x[None, :], force, table) for c in chunks]

    def combined(at, s, outs, after=()):
        near, far = (back[at][k] if k == 0 else moved[back[at][k]] for k in (2 * s, 2 * s + 1))
        return combine(v, chunks[at], s, prefetch, base[at], near, far, outs, after)

    for k in (2, 6):
        back[1][k] = trade(sent[1][place[k]], k)
    back[1][7] = trade(hold(sent[1][place[7]], base), 7)
    outs = ()
    for s in (2, 1):
        outs = combined(0, s, outs)
    back[1][3] = trade(hold(sent[1][place[3]], outs[2:]), 3)
    back[1][1] = trade(sent[1][place[1]], 1)
    for s in (0, 3):
        outs = combined(0, s, outs)
    slabs = lax.axis_size("slab")
    mark = lax.ppermute(outs[2], "slab", [(i, (i + 1) % slabs) for i in range(slabs)])
    for s in (2, 1, 0):
        outs = combined(1, s, outs)
    outs = combined(1, 3, outs, (mark,))
    tendency, updated = (jnp.transpose(o, (0, 2, 1, 3)) for o in outs[:2])
    return tendency, updated


def general_shards(
    velocity, deriv_x, deriv_y, metric_x, metric_y, coarse_force, row_map, x_index, x_weight
):
    rows, levels, components, fine_width = velocity.shape
    flattened = velocity.reshape(rows, levels * components * fine_width)
    columns = lax.all_to_all(flattened, "row", split_axis=1, concat_axis=0, tiled=True)
    slope_columns = (
        jnp.dot(deriv_y, columns, preferred_element_type=jnp.float32) * metric_y[:, None]
    ).astype(jnp.bfloat16)
    along_y = lax.all_to_all(slope_columns, "row", split_axis=0, concat_axis=1, tiled=True).reshape(
        velocity.shape
    )
    along_x = (
        jnp.dot(
            velocity.reshape(-1, fine_width), deriv_x, preferred_element_type=jnp.float32
        ).reshape(velocity.shape)
        * metric_x
    )
    coarse_width = coarse_force.shape[3]
    portion = lax.all_gather(coarse_force, "row", axis=0, tiled=True)
    force = chosen_levels(portion, jnp.arange(portion.shape[0], dtype=jnp.int32), row_map)
    table = upsample_table(x_index, x_weight, coarse_width)
    forcing = jnp.dot(
        force.reshape(-1, coarse_width), table, preferred_element_type=jnp.float32
    ).reshape(velocity.shape)
    moving = velocity.astype(jnp.float32)
    result = forcing - (
        moving[:, :, 0:1] * along_x + moving[:, :, 1:2] * along_y.astype(jnp.float32)
    )
    return (result.astype(jnp.bfloat16), (moving + rk_weight * result).astype(jnp.bfloat16))


def solution(mesh):
    shards = ring_shards if mesh.shape["row"] == 8 else general_shards
    return jax.shard_map(
        shards,
        mesh=mesh,
        in_specs=(
            P("row", "slab", None, None),
            P(),
            P(),
            P(),
            P(),
            P("row", "slab", None, None),
            P("row"),
            P(),
            P(),
        ),
        out_specs=(P("row", "slab", None, None), P("row", "slab", None, None)),
        check_vma=False,
    )
```

```python
import functools

import jax
import jax.numpy as jnp
from jax import lax
from jax.experimental import pallas as pl
from jax.experimental.pallas import tpu as pltpu
from jax.sharding import PartitionSpec as P

rk_weight = 0.5
mib = 1024 * 1024
lanes = 128
in_flight = 8
light = pl.CostEstimate(flops=1, bytes_accessed=1, transcendentals=0)


def refine_levels(extended):
    lower = extended[:, :-1]
    middle = (0.5 * (lower.astype(jnp.float32) + extended[:, 1:].astype(jnp.float32))).astype(
        jnp.bfloat16
    )
    stacked = jnp.stack([lower, middle], axis=2)
    return stacked.reshape(
        extended.shape[0], 2 * (extended.shape[1] - 1), extended.shape[2], extended.shape[3]
    )


def upsample_table(x_index, x_weight, coarse_width):
    positions = jnp.arange(coarse_width, dtype=jnp.int32)[:, None]
    nothing = jnp.zeros((), jnp.bfloat16)
    left_part = jnp.where(positions == x_index[None, :], x_weight[None, :], nothing)
    right_weight = (1.0 - x_weight.astype(jnp.float32)).astype(jnp.bfloat16)
    right_part = jnp.where(positions == x_index[None, :] + 1, right_weight[None, :], nothing)
    return left_part + right_part


def chosen_levels(portion, coarse_rows, row_map):
    selector = (row_map[:, None] == coarse_rows[None, :]).astype(jnp.bfloat16)
    chosen = (
        jnp.dot(
            selector, portion.reshape(portion.shape[0], -1), preferred_element_type=jnp.float32
        )
        .astype(jnp.bfloat16)
        .reshape((row_map.shape[0],) + portion.shape[1:])
    )
    return extended_levels(chosen)


def extended_levels(chosen):
    slabs = lax.axis_size("slab")
    route = [(i + 1, i) for i in range(slabs - 1)]
    upper_rim = lax.ppermute(chosen[:, :1], "slab", route)
    is_topmost = lax.axis_index("slab") == slabs - 1
    rim_level = jnp.where(is_topmost, chosen[:, -1:], upper_rim)
    return refine_levels(jnp.concatenate([chosen, rim_level], axis=1))


def pack_kernel(xi_ref, v_ref, *refs):
    blocks, wide = refs[-3:-1], refs[-1]
    rows, comps, levels, width = v_ref.shape
    half = levels // 2
    for c in range(comps):
        for j in range(width // lanes):
            lane = slice(j * lanes, (j + 1) * lanes)
            wide[...] = v_ref[:, c, :, lane].astype(jnp.float32).reshape(rows * levels, lanes)
            for i, block in enumerate(blocks):
                start = (xi_ref[0] ^ i) * half
                for l in range(half):
                    level = wide[pl.ds(start + l, rows, stride=levels), :]
                    block[c * half + l, :, lane] = level.astype(block.dtype)


def pack(v, comps, s, prefetch, after):
    rows, _, levels, fine_width = v.shape
    zs = prefetch.shape[0] - 1
    width = fine_width // zs
    planes = len(comps) * levels // 2
    part = rows // 2
    block = jax.ShapeDtypeStruct((2 * planes, part, width), v.dtype)
    return pl.pallas_call(
        pack_kernel,
        grid_spec=pltpu.PrefetchScalarGridSpec(
            num_scalar_prefetch=1,
            grid=(2,),
            in_specs=[
                pl.BlockSpec(
                    (part, len(comps), levels, width),
                    lambda g, xi: (g, comps[0] // len(comps), 0, xi[1 + s]),
                )
            ]
            + [pl.BlockSpec(memory_space=pl.ANY)] * len(after),
            out_specs=[pl.BlockSpec((planes, part, width), lambda g, xi: (g, 0, 0))] * 2,
            scratch_shapes=[pltpu.VMEM((part * levels, lanes), jnp.float32)],
        ),
        out_shape=[block] * 2,
        compiler_params=pltpu.CompilerParams(vmem_limit_bytes=60 * mib),
        cost_estimate=light,
        name="pack",
    )(prefetch, v, *after)


def slope_kernel(planes, places, riders, d_ref, m_ref, *refs):
    count = len(places)
    sources, results = refs[:count], refs[-count:]
    part, width = sources[0].shape[1:]
    for q in range(planes):
        columns = jnp.concatenate(
            [
                source[h * stride + start + q]
                for source, (stride, start) in zip(sources, places)
                for h in range(2)
            ],
            axis=0,
        )
        slope = jnp.dot(d_ref[...], columns, preferred_element_type=jnp.float32) * m_ref[...]
        slope = slope.astype(jnp.bfloat16)
        for k, result in enumerate(results):
            for h in range(2):
                at = (2 * k + h) * part
                result[h * planes + q] = slope[at : at + part]
    for at in riders:
        results[at][2 * planes :] = refs[count][...]


def slopes(blocks, places, planes, deriv, metric, rider=None, riders=()):
    part, width = blocks[0].shape[1:]
    count = len(blocks)
    more = [rider] if riders else []
    extra = [rider.shape[0] if at in riders else 0 for at in range(count)]
    return pl.pallas_call(
        functools.partial(slope_kernel, planes, places, riders),
        in_specs=[pl.BlockSpec(memory_space=pltpu.VMEM)] * (2 + count + len(more)),
        out_specs=[pl.BlockSpec(memory_space=pltpu.VMEM)] * count,
        out_shape=[
            jax.ShapeDtypeStruct((2 * planes + e, part, width), jnp.bfloat16) for e in extra
        ],
        compiler_params=pltpu.CompilerParams(vmem_limit_bytes=60 * mib),
        cost_estimate=light,
        name="slopes",
    )(deriv, metric, *blocks, *more)


def hold_kernel(block_ref, *refs):
    refs[-1][...] = block_ref[...]


def hold(block, after):
    return pl.pallas_call(
        hold_kernel,
        in_specs=[pl.BlockSpec(memory_space=pltpu.VMEM)]
        + [pl.BlockSpec(memory_space=pl.ANY)] * len(after),
        out_specs=pl.BlockSpec(memory_space=pltpu.VMEM),
        out_shape=jax.ShapeDtypeStruct(block.shape, block.dtype),
        compiler_params=pltpu.CompilerParams(vmem_limit_bytes=8 * mib),
        cost_estimate=light,
        name="hold",
    )(block, *after)


def choose_kernel(pick_ref, spread_ref, rider_ref, *refs):
    blocks, (levels_ref, rim_ref) = refs[:-2], refs[-2:]
    planes, part, width = rider_ref.shape
    rows = levels_ref.shape[1]
    parts = [rider_ref[...]] + [block[block.shape[0] - planes :] for block in blocks]
    source = jnp.concatenate(
        [p.astype(jnp.float32).reshape(planes * part, width) for p in parts], axis=0
    ).astype(jnp.bfloat16)
    chosen = jnp.dot(pick_ref[...], source, preferred_element_type=jnp.float32)
    chosen = chosen.astype(jnp.bfloat16)
    count = spread_ref.shape[0]
    pieces = pick_ref.shape[0] // rows
    for u in range(pieces):
        for h in range(count):
            level = jnp.dot(
                chosen[u * rows : (u + 1) * rows],
                spread_ref[h],
                preferred_element_type=jnp.float32,
            ).astype(jnp.bfloat16)
            levels_ref[u * count + h] = level
            if h == 0 and u % (pieces // rim_ref.shape[0]) == 0:
                rim_ref[u // (pieces // rim_ref.shape[0])] = level


def choose(pick, spread, rider, blocks, components):
    count, _, wide = spread.shape
    rows = 2 * rider.shape[1]
    pieces = pick.shape[0] // rows
    whole = pl.BlockSpec(memory_space=pltpu.VMEM)
    return pl.pallas_call(
        choose_kernel,
        in_specs=[whole] * (3 + len(blocks)),
        out_specs=[whole] * 2,
        out_shape=[
            jax.ShapeDtypeStruct((pieces * count, rows, wide), jnp.bfloat16),
            jax.ShapeDtypeStruct((components, rows, wide), jnp.bfloat16),
        ],
        compiler_params=pltpu.CompilerParams(vmem_limit_bytes=32 * mib),
        cost_estimate=light,
        name="choose",
    )(pick, spread, rider, *blocks)


def refine_kernel(top_ref, levels_ref, rim_ref, force_ref, wide):
    components, rows, fine, width = force_ref.shape
    coarse = fine // 2
    for c in range(components):
        level = [levels_ref[c * coarse + m].astype(jnp.float32) for m in range(coarse)]
        above = rim_ref[c].astype(jnp.float32)
        level.append(jnp.where(top_ref[0] == 1, level[-1], above))
        for j in range(width // lanes):
            lane = slice(j * lanes, (j + 1) * lanes)
            for m in range(coarse):
                low, high = level[m][:, lane], level[m + 1][:, lane]
                wide[pl.ds(2 * m, rows, stride=fine), :] = low
                middle = (0.5 * (low + high)).astype(jnp.bfloat16).astype(jnp.float32)
                wide[pl.ds(2 * m + 1, rows, stride=fine), :] = middle
            force_ref[c, :, :, lane] = (
                wide[...].reshape(rows, fine, lanes).astype(jnp.bfloat16)
            )


def refine(levels, rim, is_topmost):
    components, rows, width = rim.shape
    fine = 2 * levels.shape[0] // components
    whole = pl.BlockSpec(memory_space=pltpu.VMEM)
    return pl.pallas_call(
        refine_kernel,
        in_specs=[pl.BlockSpec(memory_space=pltpu.SMEM), whole, whole],
        out_specs=whole,
        out_shape=jax.ShapeDtypeStruct((components, rows, fine, width), jnp.bfloat16),
        scratch_shapes=[pltpu.VMEM((rows * fine, lanes), jnp.float32)],
        compiler_params=pltpu.CompilerParams(vmem_limit_bytes=32 * mib),
        cost_estimate=light,
        name="refine",
    )(is_topmost.astype(jnp.int32)[None], levels, rim)


def base_kernel(v_ref, v0_ref, d_ref, m_ref, f_ref, t_ref, base_ref):
    rows, levels, width = v_ref.shape
    flat = v_ref[...].astype(jnp.float32).reshape(rows * levels, width).astype(jnp.bfloat16)
    along = jnp.dot(flat, d_ref[...], preferred_element_type=jnp.float32) * m_ref[...]
    force = f_ref[...].astype(jnp.float32).reshape(rows * levels, -1).astype(jnp.bfloat16)
    forcing = jnp.dot(force, t_ref[...], preferred_element_type=jnp.float32)
    carry = v0_ref[...].astype(jnp.float32).reshape(rows * levels, width)
    base_ref[...] = (forcing - carry * along).reshape(rows, levels, width)


def bases(v, comps, deriv_x, metric_x, force, table):
    rows, _, levels, width = v.shape
    part = 32
    coarse_width = table.shape[0]
    first = comps[0]
    return pl.pallas_call(
        base_kernel,
        grid=(rows // part, len(comps)),
        in_specs=[
            pl.BlockSpec((part, None, levels, width), lambda g, c: (g, first + c, 0, 0)),
            pl.BlockSpec((part, None, levels, width), lambda g, c: (g, 0, 0, 0)),
            pl.BlockSpec(deriv_x.shape, lambda g, c: (0, 0)),
            pl.BlockSpec(metric_x.shape, lambda g, c: (0, 0)),
            pl.BlockSpec((None, part, levels, coarse_width), lambda g, c: (first + c, g, 0, 0)),
            pl.BlockSpec(table.shape, lambda g, c: (0, 0)),
        ],
        out_specs=pl.BlockSpec((part, None, levels, width), lambda g, c: (g, c, 0, 0)),
        out_shape=jax.ShapeDtypeStruct((rows, len(comps), levels, width), jnp.float32),
        compiler_params=pltpu.CompilerParams(vmem_limit_bytes=32 * mib),
        cost_estimate=light,
        name="bases",
    )(v, v, deriv_x, metric_x, force, table)


def combine_kernel(xi_ref, base_ref, v_ref, v1_ref, near_ref, far_ref, *refs):
    t_ref, u_ref, mark_ref, along = refs[-4:]
    mark_ref[...] = jnp.zeros(mark_ref.shape, mark_ref.dtype)
    rows, levels, width = base_ref.shape
    half = levels // 2
    for j in range(width // lanes):
        lane = slice(j * lanes, (j + 1) * lanes)
        for i, block in enumerate((near_ref, far_ref)):
            start = (xi_ref[0] ^ i) * half
            for l in range(half):
                plane = block[l, :, lane].astype(jnp.float32)
                along[pl.ds(start + l, rows, stride=levels), :] = plane
        along_y = along[...].reshape(rows, levels, lanes)
        t = base_ref[:, :, lane] - v1_ref[:, :, lane].astype(jnp.float32) * along_y
        t_ref[:, :, lane] = t.astype(jnp.bfloat16)
        moved = v_ref[:, :, lane].astype(jnp.float32) + rk_weight * t
        u_ref[:, :, lane] = moved.astype(jnp.bfloat16)


def combine(v, comps, s, prefetch, base, near, far, outs, after):
    rows, _, levels, fine_width = v.shape
    part, width = near.shape[1:]
    half = levels // 2
    first, count = comps[0], len(comps)
    block = (part, None, levels, width)
    column = pl.BlockSpec(block, lambda g, c, xi: (g, first + c, 0, xi[1 + s]))
    planes = pl.BlockSpec((half, part, width), lambda g, c, xi: (g * count + c, 0, 0))
    return pl.pallas_call(
        combine_kernel,
        grid_spec=pltpu.PrefetchScalarGridSpec(
            num_scalar_prefetch=1,
            grid=(rows // part, count),
            in_specs=[
                pl.BlockSpec(block, lambda g, c, xi: (g, c, 0, xi[1 + s])),
                column,
                pl.BlockSpec(block, lambda g, c, xi: (g, 1, 0, xi[1 + s])),
                planes,
                planes,
            ]
            + [pl.BlockSpec(memory_space=pl.ANY)] * len((*outs[:2], *after)),
            out_specs=[column, column, pl.BlockSpec((8, lanes), lambda g, c, xi: (0, 0))],
            scratch_shapes=[pltpu.VMEM((part * levels, lanes), jnp.float32)],
        ),
        out_shape=[jax.ShapeDtypeStruct(v.shape, v.dtype)] * 2
        + [jax.ShapeDtypeStruct((8, lanes), jnp.float32)],
        input_output_aliases={6: 0, 7: 1} if outs else {},
        compiler_params=pltpu.CompilerParams(vmem_limit_bytes=16 * mib),
        cost_estimate=light,
        name="combine",
    )(prefetch, base, v, v, near, far, *outs[:2], *after)


def ring_shards(
    velocity, deriv_x, deriv_y, metric_x, metric_y, coarse_force, row_map, x_index, x_weight
):
    rows, levels, components, fine_width = velocity.shape
    devices = lax.axis_size("row")
    zs = devices // 2
    width = fine_width // zs
    me = lax.axis_index("row").astype(jnp.int32)
    prefetch = jnp.concatenate([(me % 2)[None], (me // 2) ^ jnp.arange(zs, dtype=jnp.int32)])
    v = jnp.transpose(velocity, (0, 2, 1, 3))
    arrival = [0, 4, 5, 6, 7, 2, 3, 1]
    place = {k: at for at, k in enumerate(arrival)}
    moved, ready = [], []

    def trade(block, k):
        if ready:
            block, ready[-1] = lax.optimization_barrier((block, ready[-1]))
        if len(moved) >= in_flight:
            block, moved[-in_flight] = lax.optimization_barrier((block, moved[-in_flight]))
        ready.append(block)
        at = len(moved)
        moved.append(lax.ppermute(block, "row", [(i, i ^ k) for i in range(devices)]))
        return at

    coarse_here, coarse_levels, _, coarse_width = coarse_force.shape
    row_size = coarse_levels * components * coarse_width
    every = tuple(range(components))
    chunks = one, two = [every[2:], every[:2]]
    blocks, after = {}, ()
    for which, s in ((one, 2), (every, 1), (one, 3), (every, 0), (two, 2), (two, 3)):
        pair = pack(v, which, s, prefetch, after)
        blocks[which, 2 * s], blocks[which, 2 * s + 1] = pair
        after = pair[:1]
    landed = {(every, 0): blocks[every, 0]}
    rider = (
        jnp.transpose(coarse_force, (0, 2, 1, 3))
        .reshape(coarse_here, row_size)
        .reshape(-1, rows // 2, width)
    )
    blocks[one, 4] = jnp.concatenate([blocks[one, 4], rider], axis=0)
    steps = [
        (one, 5), (one, 4), (one, 6), (every, 2), (one, 7), (every, 3), (two, 4), (every, 1),
        (two, 5), (two, 6), (two, 7),
    ]
    partners = [me ^ k for k in arrival]
    piece = lambda a, at, axis: lax.dynamic_slice_in_dim(a, at * rows, rows, axis)
    by_column = jnp.concatenate([piece(deriv_y, at, 1) for at in partners], axis=1)
    deriv = jnp.concatenate([piece(by_column, at, 0) for at in partners], axis=0)
    metric = jnp.concatenate([piece(metric_y, at, 0) for at in partners], axis=0)[:, None]
    numbers = {}

    for step in steps:
        block = blocks[step]
        if step == (every, 2):
            block, deriv, metric = lax.optimization_barrier((block, deriv, metric))
        numbers[step] = trade(block, step[1])
    rider = jnp.concatenate([rider, moved[numbers[one, 4]][-rider.shape[0] :]], axis=0)

    def derivatives(chunk, *carried):
        names = [(every if k < 4 else chunk, k) for k in arrival]
        blocks = [landed[n] if n in landed else moved[numbers[n]] for n in names]
        half = levels // 2
        places = [
            (len(every) * half, chunk[0] * half) if k < 4 else (len(chunk) * half, 0)
            for k in arrival
        ]
        return slopes(blocks, places, len(chunk) * half, deriv, metric, *carried)

    sent = {0: derivatives(one, rider, [place[k] for k in (2, 3, 1)])}
    sent[1] = derivatives(two)
    back = {0: {0: sent[0][0]}, 1: {0: sent[1][0]}}
    for at, k in ((0, 5), (0, 4), (0, 2), (0, 6), (0, 3), (0, 1), (0, 7), (1, 4), (1, 5)):
        back[at][k] = trade(sent[at][place[k]], k)

    holders = jnp.stack([me ^ k for k in (0, 4, 2, 6, 3, 7, 1, 5)])
    pieces = row_size // width
    held = coarse_here * pieces
    names = (holders[:, None] * held + jnp.arange(held, dtype=jnp.int32)).reshape(-1)
    wanted = row_map[None, :] * pieces + jnp.arange(pieces, dtype=jnp.int32)[:, None]
    pick = (wanted.reshape(-1, 1) == names[None, :]).astype(jnp.bfloat16)
    side = width // coarse_width
    wide = -(-coarse_width // lanes) * lanes
    column = jnp.arange(wide, dtype=jnp.int32)
    source = jnp.arange(side, dtype=jnp.int32)[:, None] * coarse_width + column
    source = jnp.where(column < coarse_width, source, -1)
    spread = (
        jnp.arange(width, dtype=jnp.int32)[None, :, None] == source[:, None, :]
    ).astype(jnp.bfloat16)
    carriers = [moved[back[0][k]] for k in (2, 3, 1)]
    chosen, lowest = choose(pick, spread, rider, carriers, components)
    slabs = lax.axis_size("slab")
    rim = lax.ppermute(lowest, "slab", [(i + 1, i) for i in range(slabs - 1)])
    force = refine(chosen, rim, lax.axis_index("slab") == slabs - 1)
    table = upsample_table(x_index, x_weight, wide)
    base = [bases(v, c, deriv_x, metric_x[None, :], force, table) for c in chunks]

    def combined(at, s, outs, after=()):
        near, far = (back[at][k] if k == 0 else moved[back[at][k]] for k in (2 * s, 2 * s + 1))
        return combine(v, chunks[at], s, prefetch, base[at], near, far, outs, after)

    for k in (2, 6):
        back[1][k] = trade(sent[1][place[k]], k)
    back[1][7] = trade(hold(sent[1][place[7]], base), 7)
    outs = ()
    for s in (2, 1):
        outs = combined(0, s, outs)
    back[1][3] = trade(hold(sent[1][place[3]], outs[2:]), 3)
    back[1][1] = trade(sent[1][place[1]], 1)
    for s in (0, 3):
        outs = combined(0, s, outs)
    slabs = lax.axis_size("slab")
    mark = lax.ppermute(outs[2], "slab", [(i, (i + 1) % slabs) for i in range(slabs)])
    for s in (2, 1, 0):
        outs = combined(1, s, outs)
    outs = combined(1, 3, outs, (mark,))
    tendency, updated = (jnp.transpose(o, (0, 2, 1, 3)) for o in outs[:2])
    return tendency, updated


def general_shards(
    velocity, deriv_x, deriv_y, metric_x, metric_y, coarse_force, row_map, x_index, x_weight
):
    rows, levels, components, fine_width = velocity.shape
    flattened = velocity.reshape(rows, levels * components * fine_width)
    columns = lax.all_to_all(flattened, "row", split_axis=1, concat_axis=0, tiled=True)
    slope_columns = (
        jnp.dot(deriv_y, columns, preferred_element_type=jnp.float32) * metric_y[:, None]
    ).astype(jnp.bfloat16)
    along_y = lax.all_to_all(slope_columns, "row", split_axis=0, concat_axis=1, tiled=True).reshape(
        velocity.shape
    )
    along_x = (
        jnp.dot(
            velocity.reshape(-1, fine_width), deriv_x, preferred_element_type=jnp.float32
        ).reshape(velocity.shape)
        * metric_x
    )
    coarse_width = coarse_force.shape[3]
    portion = lax.all_gather(coarse_force, "row", axis=0, tiled=True)
    force = chosen_levels(portion, jnp.arange(portion.shape[0], dtype=jnp.int32), row_map)
    table = upsample_table(x_index, x_weight, coarse_width)
    forcing = jnp.dot(
        force.reshape(-1, coarse_width), table, preferred_element_type=jnp.float32
    ).reshape(velocity.shape)
    moving = velocity.astype(jnp.float32)
    result = forcing - (
        moving[:, :, 0:1] * along_x + moving[:, :, 1:2] * along_y.astype(jnp.float32)
    )
    return (result.astype(jnp.bfloat16), (moving + rk_weight * result).astype(jnp.bfloat16))


def solution(mesh):
    shards = ring_shards if mesh.shape["row"] == 8 else general_shards
    return jax.shard_map(
        shards,
        mesh=mesh,
        in_specs=(
            P("row", "slab", None, None),
            P(),
            P(),
            P(),
            P(),
            P("row", "slab", None, None),
            P("row"),
            P(),
            P(),
        ),
        out_specs=(P("row", "slab", None, None), P("row", "slab", None, None)),
        check_vma=False,
    )
```

```python
import functools

import jax
import jax.numpy as jnp
from jax import lax
from jax.experimental import pallas as pl
from jax.experimental.pallas import tpu as pltpu
from jax.sharding import PartitionSpec as P

rk_weight = 0.5
mib = 1024 * 1024
lanes = 128
in_flight = 8
light = pl.CostEstimate(flops=1, bytes_accessed=1, transcendentals=0)


def refine_levels(extended):
    lower = extended[:, :-1]
    middle = (0.5 * (lower.astype(jnp.float32) + extended[:, 1:].astype(jnp.float32))).astype(
        jnp.bfloat16
    )
    stacked = jnp.stack([lower, middle], axis=2)
    return stacked.reshape(
        extended.shape[0], 2 * (extended.shape[1] - 1), extended.shape[2], extended.shape[3]
    )


def upsample_table(x_index, x_weight, coarse_width):
    positions = jnp.arange(coarse_width, dtype=jnp.int32)[:, None]
    nothing = jnp.zeros((), jnp.bfloat16)
    left_part = jnp.where(positions == x_index[None, :], x_weight[None, :], nothing)
    right_weight = (1.0 - x_weight.astype(jnp.float32)).astype(jnp.bfloat16)
    right_part = jnp.where(positions == x_index[None, :] + 1, right_weight[None, :], nothing)
    return left_part + right_part


def chosen_levels(portion, coarse_rows, row_map):
    selector = (row_map[:, None] == coarse_rows[None, :]).astype(jnp.bfloat16)
    chosen = (
        jnp.dot(
            selector, portion.reshape(portion.shape[0], -1), preferred_element_type=jnp.float32
        )
        .astype(jnp.bfloat16)
        .reshape((row_map.shape[0],) + portion.shape[1:])
    )
    return extended_levels(chosen)


def extended_levels(chosen):
    slabs = lax.axis_size("slab")
    route = [(i + 1, i) for i in range(slabs - 1)]
    upper_rim = lax.ppermute(chosen[:, :1], "slab", route)
    is_topmost = lax.axis_index("slab") == slabs - 1
    rim_level = jnp.where(is_topmost, chosen[:, -1:], upper_rim)
    return refine_levels(jnp.concatenate([chosen, rim_level], axis=1))


def pack_kernel(xi_ref, v_ref, *refs):
    blocks, wide = refs[-3:-1], refs[-1]
    rows, comps, levels, width = v_ref.shape
    half = levels // 2
    for c in range(comps):
        for j in range(width // lanes):
            lane = slice(j * lanes, (j + 1) * lanes)
            wide[...] = v_ref[:, c, :, lane].astype(jnp.float32).reshape(rows * levels, lanes)
            for i, block in enumerate(blocks):
                start = (xi_ref[0] ^ i) * half
                for l in range(half):
                    level = wide[pl.ds(start + l, rows, stride=levels), :]
                    block[c * half + l, :, lane] = level.astype(block.dtype)


def pack(v, comps, s, prefetch, after):
    rows, _, levels, fine_width = v.shape
    zs = prefetch.shape[0] - 1
    width = fine_width // zs
    planes = len(comps) * levels // 2
    part = rows // 2
    block = jax.ShapeDtypeStruct((2 * planes, part, width), v.dtype)
    return pl.pallas_call(
        pack_kernel,
        grid_spec=pltpu.PrefetchScalarGridSpec(
            num_scalar_prefetch=1,
            grid=(2,),
            in_specs=[
                pl.BlockSpec(
                    (part, len(comps), levels, width),
                    lambda g, xi: (g, comps[0] // len(comps), 0, xi[1 + s]),
                )
            ]
            + [pl.BlockSpec(memory_space=pl.ANY)] * len(after),
            out_specs=[pl.BlockSpec((planes, part, width), lambda g, xi: (g, 0, 0))] * 2,
            scratch_shapes=[pltpu.VMEM((part * levels, lanes), jnp.float32)],
        ),
        out_shape=[block] * 2,
        compiler_params=pltpu.CompilerParams(vmem_limit_bytes=60 * mib),
        cost_estimate=light,
        name="pack",
    )(prefetch, v, *after)


def slope_kernel(planes, places, riders, d_ref, m_ref, *refs):
    count = len(places)
    sources, results = refs[:count], refs[-count:]
    part, width = sources[0].shape[1:]
    for q in range(planes):
        columns = jnp.concatenate(
            [
                source[h * stride + start + q]
                for source, (stride, start) in zip(sources, places)
                for h in range(2)
            ],
            axis=0,
        )
        slope = jnp.dot(d_ref[...], columns, preferred_element_type=jnp.float32) * m_ref[...]
        slope = slope.astype(jnp.bfloat16)
        for k, result in enumerate(results):
            for h in range(2):
                at = (2 * k + h) * part
                result[h * planes + q] = slope[at : at + part]
    for at in riders:
        results[at][2 * planes :] = refs[count][...]


def slopes(blocks, places, planes, deriv, metric, rider=None, riders=()):
    part, width = blocks[0].shape[1:]
    count = len(blocks)
    more = [rider] if riders else []
    extra = [rider.shape[0] if at in riders else 0 for at in range(count)]
    return pl.pallas_call(
        functools.partial(slope_kernel, planes, places, riders),
        in_specs=[pl.BlockSpec(memory_space=pltpu.VMEM)] * (2 + count + len(more)),
        out_specs=[pl.BlockSpec(memory_space=pltpu.VMEM)] * count,
        out_shape=[
            jax.ShapeDtypeStruct((2 * planes + e, part, width), jnp.bfloat16) for e in extra
        ],
        compiler_params=pltpu.CompilerParams(vmem_limit_bytes=60 * mib),
        cost_estimate=light,
        name="slopes",
    )(deriv, metric, *blocks, *more)


def hold_kernel(block_ref, *refs):
    refs[-1][...] = block_ref[...]


def hold(block, after):
    return pl.pallas_call(
        hold_kernel,
        in_specs=[pl.BlockSpec(memory_space=pltpu.VMEM)]
        + [pl.BlockSpec(memory_space=pl.ANY)] * len(after),
        out_specs=pl.BlockSpec(memory_space=pltpu.VMEM),
        out_shape=jax.ShapeDtypeStruct(block.shape, block.dtype),
        compiler_params=pltpu.CompilerParams(vmem_limit_bytes=8 * mib),
        cost_estimate=light,
        name="hold",
    )(block, *after)


def choose_kernel(pick_ref, spread_ref, rider_ref, *refs):
    blocks, (levels_ref, rim_ref) = refs[:-2], refs[-2:]
    planes, part, width = rider_ref.shape
    rows = levels_ref.shape[1]
    parts = [rider_ref[...]] + [block[block.shape[0] - planes :] for block in blocks]
    source = jnp.concatenate(
        [p.astype(jnp.float32).reshape(planes * part, width) for p in parts], axis=0
    ).astype(jnp.bfloat16)
    chosen = jnp.dot(pick_ref[...], source, preferred_element_type=jnp.float32)
    chosen = chosen.astype(jnp.bfloat16)
    count = spread_ref.shape[0]
    pieces = pick_ref.shape[0] // rows
    for u in range(pieces):
        for h in range(count):
            level = jnp.dot(
                chosen[u * rows : (u + 1) * rows],
                spread_ref[h],
                preferred_element_type=jnp.float32,
            ).astype(jnp.bfloat16)
            levels_ref[u * count + h] = level
            if h == 0 and u % (pieces // rim_ref.shape[0]) == 0:
                rim_ref[u // (pieces // rim_ref.shape[0])] = level


def choose(pick, spread, rider, blocks, components):
    count, _, wide = spread.shape
    rows = 2 * rider.shape[1]
    pieces = pick.shape[0] // rows
    whole = pl.BlockSpec(memory_space=pltpu.VMEM)
    return pl.pallas_call(
        choose_kernel,
        in_specs=[whole] * (3 + len(blocks)),
        out_specs=[whole] * 2,
        out_shape=[
            jax.ShapeDtypeStruct((pieces * count, rows, wide), jnp.bfloat16),
            jax.ShapeDtypeStruct((components, rows, wide), jnp.bfloat16),
        ],
        compiler_params=pltpu.CompilerParams(vmem_limit_bytes=32 * mib),
        cost_estimate=light,
        name="choose",
    )(pick, spread, rider, *blocks)


def refine_kernel(top_ref, levels_ref, rim_ref, force_ref, wide):
    components, rows, fine, width = force_ref.shape
    coarse = fine // 2
    for c in range(components):
        level = [levels_ref[c * coarse + m].astype(jnp.float32) for m in range(coarse)]
        above = rim_ref[c].astype(jnp.float32)
        level.append(jnp.where(top_ref[0] == 1, level[-1], above))
        for j in range(width // lanes):
            lane = slice(j * lanes, (j + 1) * lanes)
            for m in range(coarse):
                low, high = level[m][:, lane], level[m + 1][:, lane]
                wide[pl.ds(2 * m, rows, stride=fine), :] = low
                middle = (0.5 * (low + high)).astype(jnp.bfloat16).astype(jnp.float32)
                wide[pl.ds(2 * m + 1, rows, stride=fine), :] = middle
            force_ref[c, :, :, lane] = (
                wide[...].reshape(rows, fine, lanes).astype(jnp.bfloat16)
            )


def refine(levels, rim, is_topmost):
    components, rows, width = rim.shape
    fine = 2 * levels.shape[0] // components
    whole = pl.BlockSpec(memory_space=pltpu.VMEM)
    return pl.pallas_call(
        refine_kernel,
        in_specs=[pl.BlockSpec(memory_space=pltpu.SMEM), whole, whole],
        out_specs=whole,
        out_shape=jax.ShapeDtypeStruct((components, rows, fine, width), jnp.bfloat16),
        scratch_shapes=[pltpu.VMEM((rows * fine, lanes), jnp.float32)],
        compiler_params=pltpu.CompilerParams(vmem_limit_bytes=32 * mib),
        cost_estimate=light,
        name="refine",
    )(is_topmost.astype(jnp.int32)[None], levels, rim)


def base_kernel(v_ref, v0_ref, d_ref, m_ref, f_ref, t_ref, base_ref):
    rows, levels, width = v_ref.shape
    flat = v_ref[...].astype(jnp.float32).reshape(rows * levels, width).astype(jnp.bfloat16)
    along = jnp.dot(flat, d_ref[...], preferred_element_type=jnp.float32) * m_ref[...]
    force = f_ref[...].astype(jnp.float32).reshape(rows * levels, -1).astype(jnp.bfloat16)
    forcing = jnp.dot(force, t_ref[...], preferred_element_type=jnp.float32)
    carry = v0_ref[...].astype(jnp.float32).reshape(rows * levels, width)
    base_ref[...] = (forcing - carry * along).reshape(rows, levels, width)


def bases(v, comps, deriv_x, metric_x, force, table):
    rows, _, levels, width = v.shape
    part = 32
    coarse_width = table.shape[0]
    first = comps[0]
    return pl.pallas_call(
        base_kernel,
        grid=(rows // part, len(comps)),
        in_specs=[
            pl.BlockSpec((part, None, levels, width), lambda g, c: (g, first + c, 0, 0)),
            pl.BlockSpec((part, None, levels, width), lambda g, c: (g, 0, 0, 0)),
            pl.BlockSpec(deriv_x.shape, lambda g, c: (0, 0)),
            pl.BlockSpec(metric_x.shape, lambda g, c: (0, 0)),
            pl.BlockSpec((None, part, levels, coarse_width), lambda g, c: (first + c, g, 0, 0)),
            pl.BlockSpec(table.shape, lambda g, c: (0, 0)),
        ],
        out_specs=pl.BlockSpec((part, None, levels, width), lambda g, c: (g, c, 0, 0)),
        out_shape=jax.ShapeDtypeStruct((rows, len(comps), levels, width), jnp.float32),
        compiler_params=pltpu.CompilerParams(vmem_limit_bytes=32 * mib),
        cost_estimate=light,
        name="bases",
    )(v, v, deriv_x, metric_x, force, table)


def combine_kernel(xi_ref, base_ref, v_ref, v1_ref, near_ref, far_ref, *refs):
    t_ref, u_ref, mark_ref, along = refs[-4:]
    mark_ref[...] = jnp.zeros(mark_ref.shape, mark_ref.dtype)
    rows, levels, width = base_ref.shape
    half = levels // 2
    for j in range(width // lanes):
        lane = slice(j * lanes, (j + 1) * lanes)
        for i, block in enumerate((near_ref, far_ref)):
            start = (xi_ref[0] ^ i) * half
            for l in range(half):
                plane = block[l, :, lane].astype(jnp.float32)
                along[pl.ds(start + l, rows, stride=levels), :] = plane
        along_y = along[...].reshape(rows, levels, lanes)
        t = base_ref[:, :, lane] - v1_ref[:, :, lane].astype(jnp.float32) * along_y
        t_ref[:, :, lane] = t.astype(jnp.bfloat16)
        moved = v_ref[:, :, lane].astype(jnp.float32) + rk_weight * t
        u_ref[:, :, lane] = moved.astype(jnp.bfloat16)


def combine(v, comps, s, prefetch, base, near, far, outs, after):
    rows, _, levels, fine_width = v.shape
    part, width = near.shape[1:]
    half = levels // 2
    first, count = comps[0], len(comps)
    block = (part, None, levels, width)
    column = pl.BlockSpec(block, lambda g, c, xi: (g, first + c, 0, xi[1 + s]))
    planes = pl.BlockSpec((half, part, width), lambda g, c, xi: (g * count + c, 0, 0))
    return pl.pallas_call(
        combine_kernel,
        grid_spec=pltpu.PrefetchScalarGridSpec(
            num_scalar_prefetch=1,
            grid=(rows // part, count),
            in_specs=[
                pl.BlockSpec(block, lambda g, c, xi: (g, c, 0, xi[1 + s])),
                column,
                pl.BlockSpec(block, lambda g, c, xi: (g, 1, 0, xi[1 + s])),
                planes,
                planes,
            ]
            + [pl.BlockSpec(memory_space=pl.ANY)] * len((*outs[:2], *after)),
            out_specs=[column, column, pl.BlockSpec((8, lanes), lambda g, c, xi: (0, 0))],
            scratch_shapes=[pltpu.VMEM((part * levels, lanes), jnp.float32)],
        ),
        out_shape=[jax.ShapeDtypeStruct(v.shape, v.dtype)] * 2
        + [jax.ShapeDtypeStruct((8, lanes), jnp.float32)],
        input_output_aliases={6: 0, 7: 1} if outs else {},
        compiler_params=pltpu.CompilerParams(vmem_limit_bytes=16 * mib),
        cost_estimate=light,
        name="combine",
    )(prefetch, base, v, v, near, far, *outs[:2], *after)


def ring_shards(
    velocity, deriv_x, deriv_y, metric_x, metric_y, coarse_force, row_map, x_index, x_weight
):
    rows, levels, components, fine_width = velocity.shape
    devices = lax.axis_size("row")
    zs = devices // 2
    width = fine_width // zs
    me = lax.axis_index("row").astype(jnp.int32)
    prefetch = jnp.concatenate([(me % 2)[None], (me // 2) ^ jnp.arange(zs, dtype=jnp.int32)])
    v = jnp.transpose(velocity, (0, 2, 1, 3))
    arrival = [0, 4, 5, 6, 7, 2, 3, 1]
    place = {k: at for at, k in enumerate(arrival)}
    moved, ready = [], []

    def trade(block, k):
        if ready:
            block, ready[-1] = lax.optimization_barrier((block, ready[-1]))
        if len(moved) >= in_flight:
            block, moved[-in_flight] = lax.optimization_barrier((block, moved[-in_flight]))
        ready.append(block)
        at = len(moved)
        moved.append(lax.ppermute(block, "row", [(i, i ^ k) for i in range(devices)]))
        return at

    coarse_here, coarse_levels, _, coarse_width = coarse_force.shape
    row_size = coarse_levels * components * coarse_width
    every = tuple(range(components))
    chunks = one, two = [every[2:], every[:2]]
    coarse = jnp.transpose(coarse_force, (0, 2, 1, 3))
    across = lax.ppermute(coarse, "row", [(i, i ^ 4) for i in range(devices)])
    planes = lambda a: a.reshape(coarse_here, row_size).reshape(-1, rows // 2, width)
    blocks, after = {}, ()
    for which, s in ((one, 2), (every, 1), (one, 3), (every, 0), (two, 2), (two, 3)):
        pair = pack(v, which, s, prefetch, after)
        blocks[which, 2 * s], blocks[which, 2 * s + 1] = pair
        after = pair[:1]
    landed = {(every, 0): blocks[every, 0]}
    blocks[one, 7], across = lax.optimization_barrier((blocks[one, 7], across))
    steps = [
        (one, 5), (one, 4), (one, 6), (every, 2), (one, 7), (every, 3), (two, 4), (every, 1),
        (two, 5), (two, 6), (two, 7),
    ]
    partners = [me ^ k for k in arrival]
    piece = lambda a, at, axis: lax.dynamic_slice_in_dim(a, at * rows, rows, axis)
    by_column = jnp.concatenate([piece(deriv_y, at, 1) for at in partners], axis=1)
    deriv = jnp.concatenate([piece(by_column, at, 0) for at in partners], axis=0)
    metric = jnp.concatenate([piece(metric_y, at, 0) for at in partners], axis=0)[:, None]
    numbers = {}

    for step in steps:
        block = blocks[step]
        if step == (every, 2):
            block, deriv, metric = lax.optimization_barrier((block, deriv, metric))
        numbers[step] = trade(block, step[1])
    rider = jnp.concatenate([planes(coarse), planes(across)], axis=0)

    def derivatives(chunk, *carried):
        names = [(every if k < 4 else chunk, k) for k in arrival]
        blocks = [landed[n] if n in landed else moved[numbers[n]] for n in names]
        half = levels // 2
        places = [
            (len(every) * half, chunk[0] * half) if k < 4 else (len(chunk) * half, 0)
            for k in arrival
        ]
        return slopes(blocks, places, len(chunk) * half, deriv, metric, *carried)

    sent = {0: derivatives(one, rider, [place[k] for k in (2, 3, 1)])}
    sent[1] = derivatives(two)
    back = {0: {0: sent[0][0]}, 1: {0: sent[1][0]}}
    for at, k in ((0, 5), (0, 2), (0, 4), (0, 3), (0, 6), (0, 1), (0, 7), (1, 5), (1, 4)):
        back[at][k] = trade(sent[at][place[k]], k)

    holders = jnp.stack([me ^ k for k in (0, 4, 2, 6, 3, 7, 1, 5)])
    pieces = row_size // width
    held = coarse_here * pieces
    names = (holders[:, None] * held + jnp.arange(held, dtype=jnp.int32)).reshape(-1)
    wanted = row_map[None, :] * pieces + jnp.arange(pieces, dtype=jnp.int32)[:, None]
    pick = (wanted.reshape(-1, 1) == names[None, :]).astype(jnp.bfloat16)
    side = width // coarse_width
    wide = -(-coarse_width // lanes) * lanes
    column = jnp.arange(wide, dtype=jnp.int32)
    source = jnp.arange(side, dtype=jnp.int32)[:, None] * coarse_width + column
    source = jnp.where(column < coarse_width, source, -1)
    spread = (
        jnp.arange(width, dtype=jnp.int32)[None, :, None] == source[:, None, :]
    ).astype(jnp.bfloat16)
    carriers = [moved[back[0][k]] for k in (2, 3, 1)]
    chosen, lowest = choose(pick, spread, rider, carriers, components)
    slabs = lax.axis_size("slab")
    rim = lax.ppermute(lowest, "slab", [(i + 1, i) for i in range(slabs - 1)])
    force = refine(chosen, rim, lax.axis_index("slab") == slabs - 1)
    table = upsample_table(x_index, x_weight, wide)
    base = [bases(v, c, deriv_x, metric_x[None, :], force, table) for c in chunks]

    def combined(at, s, outs, after=()):
        near, far = (back[at][k] if k == 0 else moved[back[at][k]] for k in (2 * s, 2 * s + 1))
        return combine(v, chunks[at], s, prefetch, base[at], near, far, outs, after)

    for k in (2, 6):
        back[1][k] = trade(sent[1][place[k]], k)
    back[1][7] = trade(hold(sent[1][place[7]], base), 7)
    outs = ()
    for s in (2, 1):
        outs = combined(0, s, outs)
    back[1][3] = trade(hold(sent[1][place[3]], outs[2:]), 3)
    back[1][1] = trade(sent[1][place[1]], 1)
    for s in (0, 3):
        outs = combined(0, s, outs)
    slabs = lax.axis_size("slab")
    mark = lax.ppermute(outs[2], "slab", [(i, (i + 1) % slabs) for i in range(slabs)])
    for s in (2, 1, 0):
        outs = combined(1, s, outs)
    outs = combined(1, 3, outs, (mark,))
    tendency, updated = (jnp.transpose(o, (0, 2, 1, 3)) for o in outs[:2])
    return tendency, updated


def general_shards(
    velocity, deriv_x, deriv_y, metric_x, metric_y, coarse_force, row_map, x_index, x_weight
):
    rows, levels, components, fine_width = velocity.shape
    flattened = velocity.reshape(rows, levels * components * fine_width)
    columns = lax.all_to_all(flattened, "row", split_axis=1, concat_axis=0, tiled=True)
    slope_columns = (
        jnp.dot(deriv_y, columns, preferred_element_type=jnp.float32) * metric_y[:, None]
    ).astype(jnp.bfloat16)
    along_y = lax.all_to_all(slope_columns, "row", split_axis=0, concat_axis=1, tiled=True).reshape(
        velocity.shape
    )
    along_x = (
        jnp.dot(
            velocity.reshape(-1, fine_width), deriv_x, preferred_element_type=jnp.float32
        ).reshape(velocity.shape)
        * metric_x
    )
    coarse_width = coarse_force.shape[3]
    portion = lax.all_gather(coarse_force, "row", axis=0, tiled=True)
    force = chosen_levels(portion, jnp.arange(portion.shape[0], dtype=jnp.int32), row_map)
    table = upsample_table(x_index, x_weight, coarse_width)
    forcing = jnp.dot(
        force.reshape(-1, coarse_width), table, preferred_element_type=jnp.float32
    ).reshape(velocity.shape)
    moving = velocity.astype(jnp.float32)
    result = forcing - (
        moving[:, :, 0:1] * along_x + moving[:, :, 1:2] * along_y.astype(jnp.float32)
    )
    return (result.astype(jnp.bfloat16), (moving + rk_weight * result).astype(jnp.bfloat16))


def solution(mesh):
    shards = ring_shards if mesh.shape["row"] == 8 else general_shards
    return jax.shard_map(
        shards,
        mesh=mesh,
        in_specs=(
            P("row", "slab", None, None),
            P(),
            P(),
            P(),
            P(),
            P("row", "slab", None, None),
            P("row"),
            P(),
            P(),
        ),
        out_specs=(P("row", "slab", None, None), P("row", "slab", None, None)),
        check_vma=False,
    )
```

```python
import functools

import jax
import jax.numpy as jnp
from jax import lax
from jax.experimental import pallas as pl
from jax.experimental.pallas import tpu as pltpu
from jax.sharding import PartitionSpec as P

rk_weight = 0.5
mib = 1024 * 1024
lanes = 128
in_flight = 8
light = pl.CostEstimate(flops=1, bytes_accessed=1, transcendentals=0)


def refine_levels(extended):
    lower = extended[:, :-1]
    middle = (0.5 * (lower.astype(jnp.float32) + extended[:, 1:].astype(jnp.float32))).astype(
        jnp.bfloat16
    )
    stacked = jnp.stack([lower, middle], axis=2)
    return stacked.reshape(
        extended.shape[0], 2 * (extended.shape[1] - 1), extended.shape[2], extended.shape[3]
    )


def upsample_table(x_index, x_weight, coarse_width):
    positions = jnp.arange(coarse_width, dtype=jnp.int32)[:, None]
    nothing = jnp.zeros((), jnp.bfloat16)
    left_part = jnp.where(positions == x_index[None, :], x_weight[None, :], nothing)
    right_weight = (1.0 - x_weight.astype(jnp.float32)).astype(jnp.bfloat16)
    right_part = jnp.where(positions == x_index[None, :] + 1, right_weight[None, :], nothing)
    return left_part + right_part


def chosen_levels(portion, coarse_rows, row_map):
    selector = (row_map[:, None] == coarse_rows[None, :]).astype(jnp.bfloat16)
    chosen = (
        jnp.dot(
            selector, portion.reshape(portion.shape[0], -1), preferred_element_type=jnp.float32
        )
        .astype(jnp.bfloat16)
        .reshape((row_map.shape[0],) + portion.shape[1:])
    )
    return extended_levels(chosen)


def extended_levels(chosen):
    slabs = lax.axis_size("slab")
    route = [(i + 1, i) for i in range(slabs - 1)]
    upper_rim = lax.ppermute(chosen[:, :1], "slab", route)
    is_topmost = lax.axis_index("slab") == slabs - 1
    rim_level = jnp.where(is_topmost, chosen[:, -1:], upper_rim)
    return refine_levels(jnp.concatenate([chosen, rim_level], axis=1))


def pack_kernel(xi_ref, v_ref, *refs):
    blocks, wide = refs[-3:-1], refs[-1]
    rows, comps, levels, width = v_ref.shape
    half = levels // 2
    for c in range(comps):
        for j in range(width // lanes):
            lane = slice(j * lanes, (j + 1) * lanes)
            wide[...] = v_ref[:, c, :, lane].astype(jnp.float32).reshape(rows * levels, lanes)
            for i, block in enumerate(blocks):
                start = (xi_ref[0] ^ i) * half
                for l in range(half):
                    level = wide[pl.ds(start + l, rows, stride=levels), :]
                    block[c * half + l, :, lane] = level.astype(block.dtype)


def pack(v, comps, s, prefetch, after):
    rows, _, levels, fine_width = v.shape
    zs = prefetch.shape[0] - 1
    width = fine_width // zs
    planes = len(comps) * levels // 2
    part = rows // 2
    block = jax.ShapeDtypeStruct((2 * planes, part, width), v.dtype)
    return pl.pallas_call(
        pack_kernel,
        grid_spec=pltpu.PrefetchScalarGridSpec(
            num_scalar_prefetch=1,
            grid=(2,),
            in_specs=[
                pl.BlockSpec(
                    (part, len(comps), levels, width),
                    lambda g, xi: (g, comps[0] // len(comps), 0, xi[1 + s]),
                )
            ]
            + [pl.BlockSpec(memory_space=pl.ANY)] * len(after),
            out_specs=[pl.BlockSpec((planes, part, width), lambda g, xi: (g, 0, 0))] * 2,
            scratch_shapes=[pltpu.VMEM((part * levels, lanes), jnp.float32)],
        ),
        out_shape=[block] * 2,
        compiler_params=pltpu.CompilerParams(vmem_limit_bytes=60 * mib),
        cost_estimate=light,
        name="pack",
    )(prefetch, v, *after)


def slope_kernel(planes, places, riders, d_ref, m_ref, *refs):
    count = len(places)
    sources, results = refs[:count], refs[-count:]
    part, width = sources[0].shape[1:]
    for q in range(planes):
        columns = jnp.concatenate(
            [
                source[h * stride + start + q]
                for source, (stride, start) in zip(sources, places)
                for h in range(2)
            ],
            axis=0,
        )
        slope = jnp.dot(d_ref[...], columns, preferred_element_type=jnp.float32) * m_ref[...]
        slope = slope.astype(jnp.bfloat16)
        for k, result in enumerate(results):
            for h in range(2):
                at = (2 * k + h) * part
                result[h * planes + q] = slope[at : at + part]
    for at in riders:
        results[at][2 * planes :] = refs[count][...]


def slopes(blocks, places, planes, deriv, metric, rider=None, riders=()):
    part, width = blocks[0].shape[1:]
    count = len(blocks)
    more = [rider] if riders else []
    extra = [rider.shape[0] if at in riders else 0 for at in range(count)]
    return pl.pallas_call(
        functools.partial(slope_kernel, planes, places, riders),
        in_specs=[pl.BlockSpec(memory_space=pltpu.VMEM)] * (2 + count + len(more)),
        out_specs=[pl.BlockSpec(memory_space=pltpu.VMEM)] * count,
        out_shape=[
            jax.ShapeDtypeStruct((2 * planes + e, part, width), jnp.bfloat16) for e in extra
        ],
        compiler_params=pltpu.CompilerParams(vmem_limit_bytes=60 * mib),
        cost_estimate=light,
        name="slopes",
    )(deriv, metric, *blocks, *more)


def hold_kernel(block_ref, *refs):
    refs[-1][...] = block_ref[...]


def hold(block, after):
    return pl.pallas_call(
        hold_kernel,
        in_specs=[pl.BlockSpec(memory_space=pltpu.VMEM)]
        + [pl.BlockSpec(memory_space=pl.ANY)] * len(after),
        out_specs=pl.BlockSpec(memory_space=pltpu.VMEM),
        out_shape=jax.ShapeDtypeStruct(block.shape, block.dtype),
        compiler_params=pltpu.CompilerParams(vmem_limit_bytes=8 * mib),
        cost_estimate=light,
        name="hold",
    )(block, *after)


def choose_kernel(pick_ref, spread_ref, rider_ref, *refs):
    blocks, (levels_ref, rim_ref) = refs[:-2], refs[-2:]
    planes, part, width = rider_ref.shape
    rows = levels_ref.shape[1]
    parts = [rider_ref[...]] + [block[block.shape[0] - planes :] for block in blocks]
    source = jnp.concatenate(
        [p.astype(jnp.float32).reshape(planes * part, width) for p in parts], axis=0
    ).astype(jnp.bfloat16)
    chosen = jnp.dot(pick_ref[...], source, preferred_element_type=jnp.float32)
    chosen = chosen.astype(jnp.bfloat16)
    count = spread_ref.shape[0]
    pieces = pick_ref.shape[0] // rows
    for u in range(pieces):
        for h in range(count):
            level = jnp.dot(
                chosen[u * rows : (u + 1) * rows],
                spread_ref[h],
                preferred_element_type=jnp.float32,
            ).astype(jnp.bfloat16)
            levels_ref[u * count + h] = level
            if h == 0 and u % (pieces // rim_ref.shape[0]) == 0:
                rim_ref[u // (pieces // rim_ref.shape[0])] = level


def choose(pick, spread, rider, blocks, components):
    count, _, wide = spread.shape
    rows = 2 * rider.shape[1]
    pieces = pick.shape[0] // rows
    whole = pl.BlockSpec(memory_space=pltpu.VMEM)
    return pl.pallas_call(
        choose_kernel,
        in_specs=[whole] * (3 + len(blocks)),
        out_specs=[whole] * 2,
        out_shape=[
            jax.ShapeDtypeStruct((pieces * count, rows, wide), jnp.bfloat16),
            jax.ShapeDtypeStruct((components, rows, wide), jnp.bfloat16),
        ],
        compiler_params=pltpu.CompilerParams(vmem_limit_bytes=32 * mib),
        cost_estimate=light,
        name="choose",
    )(pick, spread, rider, *blocks)


def refine_kernel(top_ref, levels_ref, rim_ref, force_ref, wide):
    components, rows, fine, width = force_ref.shape
    coarse = fine // 2
    for c in range(components):
        level = [levels_ref[c * coarse + m].astype(jnp.float32) for m in range(coarse)]
        above = rim_ref[c].astype(jnp.float32)
        level.append(jnp.where(top_ref[0] == 1, level[-1], above))
        for j in range(width // lanes):
            lane = slice(j * lanes, (j + 1) * lanes)
            for m in range(coarse):
                low, high = level[m][:, lane], level[m + 1][:, lane]
                wide[pl.ds(2 * m, rows, stride=fine), :] = low
                middle = (0.5 * (low + high)).astype(jnp.bfloat16).astype(jnp.float32)
                wide[pl.ds(2 * m + 1, rows, stride=fine), :] = middle
            force_ref[c, :, :, lane] = (
                wide[...].reshape(rows, fine, lanes).astype(jnp.bfloat16)
            )


def refine(levels, rim, is_topmost):
    components, rows, width = rim.shape
    fine = 2 * levels.shape[0] // components
    whole = pl.BlockSpec(memory_space=pltpu.VMEM)
    return pl.pallas_call(
        refine_kernel,
        in_specs=[pl.BlockSpec(memory_space=pltpu.SMEM), whole, whole],
        out_specs=whole,
        out_shape=jax.ShapeDtypeStruct((components, rows, fine, width), jnp.bfloat16),
        scratch_shapes=[pltpu.VMEM((rows * fine, lanes), jnp.float32)],
        compiler_params=pltpu.CompilerParams(vmem_limit_bytes=32 * mib),
        cost_estimate=light,
        name="refine",
    )(is_topmost.astype(jnp.int32)[None], levels, rim)


def base_kernel(v_ref, v0_ref, d_ref, m_ref, f_ref, t_ref, base_ref):
    rows, levels, width = v_ref.shape
    flat = v_ref[...].astype(jnp.float32).reshape(rows * levels, width).astype(jnp.bfloat16)
    along = jnp.dot(flat, d_ref[...], preferred_element_type=jnp.float32) * m_ref[...]
    force = f_ref[...].astype(jnp.float32).reshape(rows * levels, -1).astype(jnp.bfloat16)
    forcing = jnp.dot(force, t_ref[...], preferred_element_type=jnp.float32)
    carry = v0_ref[...].astype(jnp.float32).reshape(rows * levels, width)
    base_ref[...] = (forcing - carry * along).reshape(rows, levels, width)


def bases(v, comps, deriv_x, metric_x, force, table):
    rows, _, levels, width = v.shape
    part = 32
    coarse_width = table.shape[0]
    first = comps[0]
    return pl.pallas_call(
        base_kernel,
        grid=(rows // part, len(comps)),
        in_specs=[
            pl.BlockSpec((part, None, levels, width), lambda g, c: (g, first + c, 0, 0)),
            pl.BlockSpec((part, None, levels, width), lambda g, c: (g, 0, 0, 0)),
            pl.BlockSpec(deriv_x.shape, lambda g, c: (0, 0)),
            pl.BlockSpec(metric_x.shape, lambda g, c: (0, 0)),
            pl.BlockSpec((None, part, levels, coarse_width), lambda g, c: (first + c, g, 0, 0)),
            pl.BlockSpec(table.shape, lambda g, c: (0, 0)),
        ],
        out_specs=pl.BlockSpec((part, None, levels, width), lambda g, c: (g, c, 0, 0)),
        out_shape=jax.ShapeDtypeStruct((rows, len(comps), levels, width), jnp.float32),
        compiler_params=pltpu.CompilerParams(vmem_limit_bytes=32 * mib),
        cost_estimate=light,
        name="bases",
    )(v, v, deriv_x, metric_x, force, table)


def combine_kernel(xi_ref, base_ref, v_ref, v1_ref, *refs):
    t_ref, u_ref, mark_ref, along = refs[-4:]
    mark_ref[...] = jnp.zeros(mark_ref.shape, mark_ref.dtype)
    rows, levels, width = base_ref.shape
    half = levels // 2
    for j in range(width // lanes):
        lane = slice(j * lanes, (j + 1) * lanes)
        for at, block in enumerate(refs[:4]):
            i, h = divmod(at, 2)
            part = block.shape[1]
            start = (xi_ref[0] ^ i) * half
            for l in range(half):
                plane = block[l, :, lane].astype(jnp.float32)
                first = h * part * levels + start + l
                along[pl.ds(first, part, stride=levels), :] = plane
        along_y = along[...].reshape(rows, levels, lanes)
        t = base_ref[:, :, lane] - v1_ref[:, :, lane].astype(jnp.float32) * along_y
        t_ref[:, :, lane] = t.astype(jnp.bfloat16)
        moved = v_ref[:, :, lane].astype(jnp.float32) + rk_weight * t
        u_ref[:, :, lane] = moved.astype(jnp.bfloat16)


def combine(v, comps, s, prefetch, base, near, far, outs, after):
    rows, _, levels, fine_width = v.shape
    part, width = near.shape[1:]
    half = levels // 2
    first, count = comps[0], len(comps)
    block = (rows, None, levels, width)
    column = pl.BlockSpec(block, lambda g, c, xi: (g, first + c, 0, xi[1 + s]))
    planes = [
        pl.BlockSpec((half, part, width), lambda g, c, xi, h=h: (h * count + c, 0, 0))
        for h in range(2)
    ]
    return pl.pallas_call(
        combine_kernel,
        grid_spec=pltpu.PrefetchScalarGridSpec(
            num_scalar_prefetch=1,
            grid=(1, count),
            in_specs=[
                pl.BlockSpec(block, lambda g, c, xi: (g, c, 0, xi[1 + s])),
                column,
                pl.BlockSpec(block, lambda g, c, xi: (g, 1, 0, xi[1 + s])),
            ]
            + planes * 2
            + [pl.BlockSpec(memory_space=pl.ANY)] * len((*outs[:2], *after)),
            out_specs=[column, column, pl.BlockSpec((8, lanes), lambda g, c, xi: (0, 0))],
            scratch_shapes=[pltpu.VMEM((rows * levels, lanes), jnp.float32)],
        ),
        out_shape=[jax.ShapeDtypeStruct(v.shape, v.dtype)] * 2
        + [jax.ShapeDtypeStruct((8, lanes), jnp.float32)],
        input_output_aliases={8: 0, 9: 1} if outs else {},
        compiler_params=pltpu.CompilerParams(vmem_limit_bytes=16 * mib),
        cost_estimate=light,
        name="combine",
    )(prefetch, base, v, v, near, near, far, far, *outs[:2], *after)


def ring_shards(
    velocity, deriv_x, deriv_y, metric_x, metric_y, coarse_force, row_map, x_index, x_weight
):
    rows, levels, components, fine_width = velocity.shape
    devices = lax.axis_size("row")
    zs = devices // 2
    width = fine_width // zs
    me = lax.axis_index("row").astype(jnp.int32)
    prefetch = jnp.concatenate([(me % 2)[None], (me // 2) ^ jnp.arange(zs, dtype=jnp.int32)])
    v = jnp.transpose(velocity, (0, 2, 1, 3))
    arrival = [0, 4, 5, 6, 7, 2, 3, 1]
    place = {k: at for at, k in enumerate(arrival)}
    moved, ready = [], []

    def trade(block, k):
        if ready:
            block, ready[-1] = lax.optimization_barrier((block, ready[-1]))
        if len(moved) >= in_flight:
            block, moved[-in_flight] = lax.optimization_barrier((block, moved[-in_flight]))
        ready.append(block)
        at = len(moved)
        moved.append(lax.ppermute(block, "row", [(i, i ^ k) for i in range(devices)]))
        return at

    coarse_here, coarse_levels, _, coarse_width = coarse_force.shape
    row_size = coarse_levels * components * coarse_width
    every = tuple(range(components))
    chunks = one, two = [every[2:], every[:2]]
    coarse = jnp.transpose(coarse_force, (0, 2, 1, 3))
    across = lax.ppermute(coarse, "row", [(i, i ^ 4) for i in range(devices)])
    planes = lambda a: a.reshape(coarse_here, row_size).reshape(-1, rows // 2, width)
    blocks, after = {}, ()
    for which, s in ((one, 2), (every, 1), (one, 3), (every, 0), (two, 2), (two, 3)):
        pair = pack(v, which, s, prefetch, after)
        blocks[which, 2 * s], blocks[which, 2 * s + 1] = pair
        after = pair[:1]
    landed = {(every, 0): blocks[every, 0]}
    blocks[one, 7], across = lax.optimization_barrier((blocks[one, 7], across))
    steps = [
        (one, 5), (one, 4), (one, 6), (every, 2), (one, 7), (every, 3), (two, 4), (every, 1),
        (two, 5), (two, 6), (two, 7),
    ]
    partners = [me ^ k for k in arrival]
    piece = lambda a, at, axis: lax.dynamic_slice_in_dim(a, at * rows, rows, axis)
    by_column = jnp.concatenate([piece(deriv_y, at, 1) for at in partners], axis=1)
    deriv = jnp.concatenate([piece(by_column, at, 0) for at in partners], axis=0)
    metric = jnp.concatenate([piece(metric_y, at, 0) for at in partners], axis=0)[:, None]
    numbers = {}

    for step in steps:
        block = blocks[step]
        if step == (every, 2):
            block, deriv, metric = lax.optimization_barrier((block, deriv, metric))
        numbers[step] = trade(block, step[1])
    rider = jnp.concatenate([planes(coarse), planes(across)], axis=0)

    def derivatives(chunk, *carried):
        names = [(every if k < 4 else chunk, k) for k in arrival]
        blocks = [landed[n] if n in landed else moved[numbers[n]] for n in names]
        half = levels // 2
        places = [
            (len(every) * half, chunk[0] * half) if k < 4 else (len(chunk) * half, 0)
            for k in arrival
        ]
        return slopes(blocks, places, len(chunk) * half, deriv, metric, *carried)

    sent = {0: derivatives(one, rider, [place[k] for k in (2, 3, 1)])}
    sent[1] = derivatives(two)
    back = {0: {0: sent[0][0]}, 1: {0: sent[1][0]}}
    for at, k in ((0, 5), (0, 2), (0, 4), (0, 3), (0, 6), (0, 1), (0, 7), (1, 5), (1, 4)):
        back[at][k] = trade(sent[at][place[k]], k)

    holders = jnp.stack([me ^ k for k in (0, 4, 2, 6, 3, 7, 1, 5)])
    pieces = row_size // width
    held = coarse_here * pieces
    names = (holders[:, None] * held + jnp.arange(held, dtype=jnp.int32)).reshape(-1)
    wanted = row_map[None, :] * pieces + jnp.arange(pieces, dtype=jnp.int32)[:, None]
    pick = (wanted.reshape(-1, 1) == names[None, :]).astype(jnp.bfloat16)
    side = width // coarse_width
    wide = -(-coarse_width // lanes) * lanes
    column = jnp.arange(wide, dtype=jnp.int32)
    source = jnp.arange(side, dtype=jnp.int32)[:, None] * coarse_width + column
    source = jnp.where(column < coarse_width, source, -1)
    spread = (
        jnp.arange(width, dtype=jnp.int32)[None, :, None] == source[:, None, :]
    ).astype(jnp.bfloat16)
    carriers = [moved[back[0][k]] for k in (2, 3, 1)]
    chosen, lowest = choose(pick, spread, rider, carriers, components)
    slabs = lax.axis_size("slab")
    rim = lax.ppermute(lowest, "slab", [(i + 1, i) for i in range(slabs - 1)])
    force = refine(chosen, rim, lax.axis_index("slab") == slabs - 1)
    table = upsample_table(x_index, x_weight, wide)
    base = [bases(v, c, deriv_x, metric_x[None, :], force, table) for c in chunks]

    def combined(at, s, outs, after=()):
        near, far = (back[at][k] if k == 0 else moved[back[at][k]] for k in (2 * s, 2 * s + 1))
        return combine(v, chunks[at], s, prefetch, base[at], near, far, outs, after)

    for k in (2, 6):
        back[1][k] = trade(sent[1][place[k]], k)
    back[1][7] = trade(hold(sent[1][place[7]], base), 7)
    outs = ()
    for s in (2, 1):
        outs = combined(0, s, outs)
    back[1][3] = trade(hold(sent[1][place[3]], outs[2:]), 3)
    back[1][1] = trade(sent[1][place[1]], 1)
    for s in (0, 3):
        outs = combined(0, s, outs)
    slabs = lax.axis_size("slab")
    mark = lax.ppermute(outs[2], "slab", [(i, (i + 1) % slabs) for i in range(slabs)])
    for s in (2, 1, 0):
        outs = combined(1, s, outs)
    outs = combined(1, 3, outs, (mark,))
    tendency, updated = (jnp.transpose(o, (0, 2, 1, 3)) for o in outs[:2])
    return tendency, updated


def general_shards(
    velocity, deriv_x, deriv_y, metric_x, metric_y, coarse_force, row_map, x_index, x_weight
):
    rows, levels, components, fine_width = velocity.shape
    flattened = velocity.reshape(rows, levels * components * fine_width)
    columns = lax.all_to_all(flattened, "row", split_axis=1, concat_axis=0, tiled=True)
    slope_columns = (
        jnp.dot(deriv_y, columns, preferred_element_type=jnp.float32) * metric_y[:, None]
    ).astype(jnp.bfloat16)
    along_y = lax.all_to_all(slope_columns, "row", split_axis=0, concat_axis=1, tiled=True).reshape(
        velocity.shape
    )
    along_x = (
        jnp.dot(
            velocity.reshape(-1, fine_width), deriv_x, preferred_element_type=jnp.float32
        ).reshape(velocity.shape)
        * metric_x
    )
    coarse_width = coarse_force.shape[3]
    portion = lax.all_gather(coarse_force, "row", axis=0, tiled=True)
    force = chosen_levels(portion, jnp.arange(portion.shape[0], dtype=jnp.int32), row_map)
    table = upsample_table(x_index, x_weight, coarse_width)
    forcing = jnp.dot(
        force.reshape(-1, coarse_width), table, preferred_element_type=jnp.float32
    ).reshape(velocity.shape)
    moving = velocity.astype(jnp.float32)
    result = forcing - (
        moving[:, :, 0:1] * along_x + moving[:, :, 1:2] * along_y.astype(jnp.float32)
    )
    return (result.astype(jnp.bfloat16), (moving + rk_weight * result).astype(jnp.bfloat16))


def solution(mesh):
    shards = ring_shards if mesh.shape["row"] == 8 else general_shards
    return jax.shard_map(
        shards,
        mesh=mesh,
        in_specs=(
            P("row", "slab", None, None),
            P(),
            P(),
            P(),
            P(),
            P("row", "slab", None, None),
            P("row"),
            P(),
            P(),
        ),
        out_specs=(P("row", "slab", None, None), P("row", "slab", None, None)),
        check_vma=False,
    )
```
